32 devices in a mesh: dp: 4 (over y, x), ctx: 8 (over z, core).
Axes of the slice: x: 2, y: 2, z: 4, core: 2. Of those that a mesh axis runs over, the one named last changes fastest.
Arguments:
- queries: bfloat16 [6144, 4096], P(('dp', 'ctx')), may hold values from -6.5 to 6.5
- keys: bfloat16 [6144, 512], P(('dp', 'ctx')), may hold values from -4 to 4
- values: bfloat16 [6144, 512], P(('dp', 'ctx')), may hold values from -6 to 6
- out_grad: bfloat16 [6144, 4096], P(('dp', 'ctx')), may hold values from -6 to 6
- hidden: bfloat16 [6144, 8192], P(('dp', 'ctx')), may hold values from -6 to 6
Outputs:
- query_grad: bfloat16 [6144, 4096], P(('dp', 'ctx'))
- key_grad: bfloat16 [6144, 512], P(('dp', 'ctx'))
- value_grad: bfloat16 [6144, 512], P(('dp', 'ctx'))
- key_weight_grad: float32 [8192, 512], P(('dp', 'ctx'))
- value_weight_grad: float32 [8192, 512], P(('dp', 'ctx'))
The draws below stay inside these ranges and needn't reach their ends.
All inputs are finite; a program needn't handle non-finite values.
Results may differ from the reference program's by a relative error of at most 0.02.
Values may be sent and summed in bfloat16 or wider, within the bound.
No kernel may reach another device: no remote copies, remote signals or barrier semaphores. Data moves between devices by JAX's collectives and lax.ppermute only.
A program may use at most 256 MiB of HBM per device.

```python
import math
import jax
import jax.numpy as jnp
from jax import lax

D = 8192
QH = 32
KVH = 4
HD = 128
SEQ = 1536
TOKENS = 6144
QPD = 4
REPL = 2
N_DP = 4


def draw_queries(key, part):
    shape = (TOKENS, QH * HD)
    base = jnp.clip(jax.random.normal(jax.random.fold_in(key, 1), shape, jnp.float32), -4.0, 4.0)
    return base.astype(jnp.bfloat16)


def draw_keys(key, part):
    shape = (TOKENS, KVH * HD)
    base = jnp.clip(jax.random.normal(jax.random.fold_in(key, 2), shape, jnp.float32), -4.0, 4.0)
    return base.astype(jnp.bfloat16)


def spiked(drawn, own_key, source, target, parts, factor):
    def block_of(dim):
        return (jnp.arange(drawn.shape[dim]) // (drawn.shape[dim] // parts)).reshape((-1,) + (1,) * (drawn.ndim - 1 - dim))

    first = jax.random.permutation(own_key, parts)[block_of(target)]
    second = (block_of(target) + parts // 2) % parts
    return jnp.where((block_of(source) == first) | (block_of(source) == second), factor * drawn, drawn)


def block_levels(rng, extent, shards, low, largest):
    factor_of, own = 1.0, jax.random.fold_in(rng, 6)
    for axis_at, blocks in shards:
        draws = jnp.exp(jax.random.uniform(jax.random.fold_in(own, axis_at), (blocks,), jnp.float32, low / len(shards), largest / len(shards)))
        factor_of = factor_of * jnp.repeat(draws, extent[axis_at] // blocks).reshape([-1 if axis == axis_at else 1 for axis in range(len(extent))])
    return factor_of


def scatter_about(rng, dims, deviation, most, pieces=(), kind=jnp.bfloat16):
    values = deviation * jax.random.normal(rng, dims, jnp.float32)
    if pieces:
        values = values * block_levels(rng, dims, pieces, -0.22, 0.18)
    return jnp.clip(values, -most, most).astype(kind)


def bell_draw_with(rng, shape, spread, reach, shards, heavy, held_as=jnp.bfloat16):
    drawn = spread * jax.random.normal(rng, shape, jnp.float32)
    if shards:
        drawn = drawn * block_levels(rng, shape, shards, -0.22, 0.18)
    return jnp.clip(spiked(drawn, jax.random.fold_in(rng, 3), *heavy), -reach, reach).astype(held_as)


def setup_inputs(seed: int = 0) -> dict:
    splits = jax.random.split(jax.random.key(seed), 6)
    queries = draw_queries(jax.random.fold_in(splits[5], 71), 0)
    keys = draw_keys(jax.random.fold_in(splits[5], 71), 0)
    values = scatter_about(splits[2], (TOKENS, KVH * HD), 1.0, 6.0, ((0, 32),))
    out_grad = scatter_about(splits[3], (TOKENS, QH * HD), 1.0, 6.0, ((0, 32),))
    hidden = bell_draw_with(splits[4], (TOKENS, D), 1.0, 6.0, ((0, 32),), (0, 1, 32, 2.75))
    return {"queries": queries, "keys": keys, "values": values, "out_grad": out_grad, "hidden": hidden}


def head_backward(inputs):
    query, key_row, value_row, grad_out = inputs
    score_scale = 1.0 / math.sqrt(HD)
    scores = jnp.dot(query, key_row.T, preferred_element_type=jnp.float32) * score_scale
    row_ids = lax.broadcasted_iota(jnp.int32, scores.shape, 0)
    col_ids = lax.broadcasted_iota(jnp.int32, scores.shape, 1)
    scores = jnp.where(col_ids <= row_ids, scores, -jnp.inf)
    row_max = lax.optimization_barrier(jnp.max(scores, axis=1, keepdims=True))
    exponent = jnp.exp(scores - row_max)
    probability = exponent / lax.optimization_barrier(jnp.sum(exponent, axis=1, keepdims=True))
    prob_low = probability.astype(jnp.bfloat16)
    attended = jnp.dot(prob_low, value_row, preferred_element_type=jnp.float32)
    row_delta = lax.optimization_barrier(jnp.sum(grad_out.astype(jnp.float32) * attended, axis=1, keepdims=True))
    prob_grad = jnp.dot(grad_out, value_row.T, preferred_element_type=jnp.float32)
    score_grad = (probability * (prob_grad - row_delta)).astype(jnp.bfloat16)
    query_grad = (jnp.dot(score_grad, key_row, preferred_element_type=jnp.float32) * score_scale).astype(jnp.bfloat16)
    key_grad = jnp.dot(score_grad.T, query, preferred_element_type=jnp.float32) * score_scale
    value_grad = jnp.dot(prob_low.T, grad_out, preferred_element_type=jnp.float32)
    return (query_grad, key_grad, value_grad)

def combine_heads(per_head):
    partial_value = lax.optimization_barrier(jnp.sum(per_head.reshape(KVH, REPL, QPD, SEQ, HD), axis=2)).astype(jnp.bfloat16)
    total = lax.optimization_barrier(jnp.sum(partial_value.astype(jnp.float32), axis=1)).astype(jnp.bfloat16)
    return total.transpose(1, 0, 2).reshape(SEQ, KVH * HD)

def sequence_backward(inputs):
    query_seq, key_seq, value_seq, grad_seq = inputs
    group = QH // KVH
    query_heads = query_seq.reshape(SEQ, QH, HD).transpose(1, 0, 2)
    grad_heads = grad_seq.reshape(SEQ, QH, HD).transpose(1, 0, 2)
    key_heads = jnp.repeat(key_seq.reshape(SEQ, KVH, HD).transpose(1, 0, 2), group, axis=0)
    value_heads = jnp.repeat(value_seq.reshape(SEQ, KVH, HD).transpose(1, 0, 2), group, axis=0)
    query_grad, key_grad, value_grad = lax.map(head_backward, (query_heads, key_heads, value_heads, grad_heads))
    query_grad = query_grad.transpose(1, 0, 2).reshape(SEQ, QH * HD)
    return (query_grad, combine_heads(key_grad), combine_heads(value_grad))

def reference(queries, keys, values, out_grad, hidden):
    query_grad, key_grad, value_grad = lax.map(sequence_backward, (queries.reshape(N_DP, SEQ, QH * HD), keys.reshape(N_DP, SEQ, KVH * HD), values.reshape(N_DP, SEQ, KVH * HD), out_grad.reshape(N_DP, SEQ, QH * HD)))
    query_grad = query_grad.reshape(TOKENS, QH * HD)
    key_grad = key_grad.reshape(TOKENS, KVH * HD)
    value_grad = value_grad.reshape(TOKENS, KVH * HD)
    contract = (((0,), (0,)), ((), ()))
    key_weight_grad = lax.dot_general(hidden, key_grad, contract, preferred_element_type=jnp.float32)
    value_weight_grad = lax.dot_general(hidden, value_grad, contract, preferred_element_type=jnp.float32)
    return (query_grad, key_grad, value_grad, key_weight_grad, value_weight_grad)
```

```python
import functools
import math

import jax
import jax.numpy as jnp
from jax import lax
from jax.experimental import pallas as pl
from jax.experimental.pallas import tpu as pltpu
from jax.sharding import PartitionSpec as P

HD = 128
PAIR = 2
F32, BF16 = jnp.float32, jnp.bfloat16
NT = (((1,), (1,)), ((), ()))
TN = (((0,), (0,)), ((), ()))


def xor_permute(array, axis, size, mask):
    return lax.ppermute(array, axis, [(i, i ^ mask) for i in range(size)])


def attention_kernel(
    chips, tok, group, head, pos_ref, q_own, q_rx, g_own, g_rx, *refs
):
    kv_in = refs[:chips]
    dq_own, dq_oth = refs[chips : chips + 2]
    dkv_out = refs[chips + 2 : 2 * chips + 2]
    qs, gs, kv, acc, es, ds, ms, dqa, dqs, sems = refs[2 * chips + 2 :]
    span = PAIR * tok
    rows = PAIR * span
    width = group * HD
    chip, core = pos_ref[0], pos_ref[1]
    heads = q_own.shape[1] // (PAIR * width)
    col = pl.multiple_of((core * heads + head) * width, width)
    own = pl.multiple_of(core * tok, tok)
    oth = pl.multiple_of((1 - core) * tok, tok)
    copies = [
        (q_own.at[:, pl.ds(col, width)], qs.at[pl.ds(own, tok)]),
        (q_rx, qs.at[pl.ds(oth, tok)]),
        (g_own.at[:, pl.ds(col, width)], gs.at[pl.ds(own, tok)]),
        (g_rx, gs.at[pl.ds(oth, tok)]),
    ] + [
        (kv_in[s], kv.at[pl.ds(pl.multiple_of((chip ^ s) * span, span), span)])
        for s in range(chips)
    ]
    started = [pltpu.make_async_copy(a, b, sems.at[i]) for i, (a, b) in enumerate(copies)]
    for c in started:
        c.start()
    acc[...] = jnp.zeros_like(acc)
    for c in started:
        c.wait()
    scale = 1.0 / math.sqrt(HD)
    log_scale = scale * math.log2(math.e)

    def two_heads(ref, u):
        both = ref[:, pl.ds(pl.multiple_of(u * PAIR * HD, PAIR * HD), PAIR * HD)]
        return jnp.concatenate([both[:, i * HD : (i + 1) * HD] for i in range(PAIR)], 0)

    def unit(u, _):
        q = two_heads(qs, u)
        g = two_heads(gs, u)

        def scores(j, carry, masked):
            top, total, weighted = carry
            at = pl.ds(pl.multiple_of(j * span, span), span)
            s = lax.dot_general(kv[at, :HD], q, NT, preferred_element_type=F32) * log_scale
            if masked:
                key_ids = lax.broadcasted_iota(jnp.int32, (span, span), 0)
                row_ids = lax.broadcasted_iota(jnp.int32, (span, span), 1)
                keep = key_ids <= row_ids
                s = jnp.concatenate(
                    [jnp.where(keep, s[:, i * span : (i + 1) * span], -jnp.inf) for i in range(PAIR)], 1
                )
            dp = lax.dot_general(kv[at, HD:], g, NT, preferred_element_type=F32)
            new = jnp.maximum(top, jnp.max(s, axis=0, keepdims=True))
            e = jnp.exp2(s - new)
            fade = jnp.exp2(top - new)
            es[j] = e
            ds[j] = dp
            ms[j] = new
            return (
                new,
                total * fade + jnp.sum(e, axis=0, keepdims=True),
                weighted * fade + jnp.sum(e * dp, axis=0, keepdims=True),
            )

        zero = jnp.zeros((1, rows), F32)
        carry = scores(chip, (jnp.full((1, rows), -jnp.inf, F32), zero, zero), True)
        top, total, weighted = lax.fori_loop(
            0, chip, lambda j, c: scores(j, c, False), carry
        )
        inv = 1.0 / total
        delta = weighted * inv
        dqa[...] = jnp.zeros_like(dqa)

        def grads(j, _):
            at = pl.ds(pl.multiple_of(j * span, span), span)
            p = es[j] * (jnp.exp2(ms[j] - top) * inv)
            sg = (p * (ds[j] - delta)).astype(BF16)
            acc[at, HD:] += jnp.dot(p.astype(BF16), g, preferred_element_type=F32)
            acc[at, :HD] += jnp.dot(sg, q, preferred_element_type=F32)
            dqa[...] += lax.dot_general(sg, kv[at, :HD], TN, preferred_element_type=F32)
            return 0

        lax.fori_loop(0, chip + 1, grads, 0)
        out = (dqa[...] * scale).astype(BF16)
        dqs[:, pl.ds(pl.multiple_of(u * PAIR * HD, PAIR * HD), PAIR * HD)] = jnp.concatenate(
            [out[i * span : (i + 1) * span] for i in range(PAIR)], 1
        )
        return 0

    lax.fori_loop(0, group // PAIR, unit, 0)
    dq_own[...] = dqs[pl.ds(own, tok), :]
    dq_oth[...] = dqs[pl.ds(oth, tok), :]
    for s in range(chips):
        j = chip ^ s
        at = pl.ds(pl.multiple_of(j * span, span), span)
        out = dkv_out[s]

        @pl.when(j <= chip)
        def _():
            out[:, :HD] = (acc[at, :HD] * scale).astype(out.dtype)
            out[:, HD:] = acc[at, HD:].astype(out.dtype)

        @pl.when(j > chip)
        def _():
            out[...] = jnp.zeros_like(out)


def attention(pos, q_own, q_rx, g_own, g_rx, kv_slots, head):
    chips = len(kv_slots)
    span = kv_slots[0].shape[0]
    tok = span // PAIR
    width = q_rx.shape[1]
    group = width // HD
    rows = PAIR * span
    anywhere = pl.BlockSpec(memory_space=pl.ANY)
    vmem = pl.BlockSpec(memory_space=pltpu.VMEM)
    out_shape = [jax.ShapeDtypeStruct((tok, width), BF16)] * 2 + [
        jax.ShapeDtypeStruct((span, 2 * HD), BF16 if s else F32) for s in range(chips)
    ]
    cells = width // HD * span * (chips + 1) * span // 2
    outs = pl.pallas_call(
        functools.partial(attention_kernel, chips, tok, group, head),
        out_shape=out_shape,
        in_specs=[pl.BlockSpec(memory_space=pltpu.SMEM)] + [anywhere] * (4 + chips),
        out_specs=[vmem] * (2 + chips),
        scratch_shapes=[
            pltpu.VMEM((span, width), BF16),
            pltpu.VMEM((span, width), BF16),
            pltpu.VMEM((chips * span, 2 * HD), BF16),
            pltpu.VMEM((chips * span, 2 * HD), F32),
            pltpu.VMEM((chips, span, rows), F32),
            pltpu.VMEM((chips, span, rows), F32),
            pltpu.VMEM((chips, 1, rows), F32),
            pltpu.VMEM((rows, HD), F32),
            pltpu.VMEM((span, width), BF16),
            pltpu.SemaphoreType.DMA((4 + chips,)),
        ],
        compiler_params=pltpu.CompilerParams(vmem_limit_bytes=44 * 1024 * 1024),
        cost_estimate=pl.CostEstimate(
            flops=10 * cells * HD, bytes_accessed=6 * span * width, transcendentals=cells
        ),
        name="attention_grads",
    )(pos, q_own, q_rx, g_own, g_rx, *kv_slots)
    return outs[0], outs[1], outs[2:]


def on_device(queries, keys, values, out_grad, hidden):
    tok = queries.shape[0]
    n_dp, n_ctx = lax.axis_size("dp"), lax.axis_size("ctx")
    chips = n_ctx // PAIR
    kv_heads = keys.shape[1] // HD
    own_heads = kv_heads // PAIR
    width = queries.shape[1] // kv_heads
    dp, ctx = lax.axis_index("dp"), lax.axis_index("ctx")
    chip, core = ctx // PAIR, ctx % PAIR
    pos = jnp.stack([chip, core]).astype(jnp.int32)
    first = core == 0

    def swap(x):
        return xor_permute(x, "ctx", n_ctx, 1)

    def across(x, mask):
        return xor_permute(x, "ctx", n_ctx, mask * PAIR)

    def in_order(mine, theirs, axis):
        return jnp.where(
            first,
            jnp.concatenate([mine, theirs], axis),
            jnp.concatenate([theirs, mine], axis),
        )

    def columns(x, head, size):
        return lax.dynamic_slice_in_dim(x, head * size, size, 1)

    def gather_kv(a):
        mine = core * own_heads + a
        theirs = (1 - core) * own_heads + a
        kept = jnp.concatenate([columns(keys, mine, HD), columns(values, mine, HD)], 1)
        sent = jnp.concatenate([columns(keys, theirs, HD), columns(values, theirs, HD)], 1)
        slots = {0: in_order(kept, swap(sent), 0)}
        bit = chips // 2
        while bit:
            slots.update({s ^ bit: across(x, bit) for s, x in slots.items()})
            bit //= 2
        return [slots[s] for s in range(chips)]

    def reduce_blocks(blocks):
        cur = dict(enumerate(blocks))
        bit = 1
        while bit < chips:
            for s in [s for s in cur if s & bit]:
                got = across(cur.pop(s).astype(BF16), bit)
                cur[s ^ bit] = cur[s ^ bit].astype(F32) + got.astype(F32)
            bit *= 2
        return cur[0]

    share = hidden.shape[1] // n_dp
    parts = [columns(hidden, dp, share)] + [
        xor_permute(columns(hidden, dp ^ s, share), "dp", n_dp, s) for s in range(1, n_dp)
    ]
    hidden_own = jnp.concatenate(parts, 0)
    hidden_oth = swap(hidden_own)

    query_own, query_oth, key_value, weights = [], [], [], []
    for a in range(own_heads):
        theirs = (1 - core) * own_heads + a
        q_rx = swap(columns(queries, theirs, width))
        g_rx = swap(columns(out_grad, theirs, width))
        kv_slots = gather_kv(a)
        dq_own, dq_oth, blocks = attention(pos, queries, q_rx, out_grad, g_rx, kv_slots, a)
        query_own.append(dq_own)
        query_oth.append(swap(dq_oth))
        total = reduce_blocks(blocks).astype(BF16)
        total = jnp.where(first, total, jnp.concatenate([total[tok:], total[:tok]], 0))
        key_value.append((total[:tok], swap(total[tok:])))
        every = [total] + [xor_permute(total, "dp", n_dp, s) for s in range(1, n_dp)]
        kv_own = jnp.concatenate([x[:tok] for x in every], 0)
        kv_oth = jnp.concatenate([x[tok:] for x in every], 0)
        product = lax.dot_general(
            hidden_own, kv_own, TN, preferred_element_type=F32
        ) + lax.dot_general(hidden_oth, kv_oth, TN, preferred_element_type=F32)
        product = product.astype(BF16).reshape(chips, share // chips, 2 * HD)
        summed = reduce_blocks(
            [lax.dynamic_index_in_dim(product, chip ^ s, 0, False) for s in range(chips)]
        ).astype(F32)
        rows = share // n_ctx
        mine = lax.dynamic_slice_in_dim(summed, core * rows, rows, 0)
        theirs = lax.dynamic_slice_in_dim(summed, (1 - core) * rows, rows, 0)
        weights.append((mine, swap(theirs)))

    def spread(pairs, lo):
        mine = jnp.concatenate([m[:, lo : lo + HD] for m, _ in pairs], 1)
        theirs = jnp.concatenate([t[:, lo : lo + HD] for _, t in pairs], 1)
        return in_order(mine, theirs, 1)

    query_grad = in_order(
        jnp.concatenate(query_own, 1), jnp.concatenate(query_oth, 1), 1
    )
    return (
        query_grad,
        spread(key_value, 0),
        spread(key_value, HD),
        spread(weights, 0),
        spread(weights, HD),
    )


def solution(mesh):
    spec = P(("dp", "ctx"), None)
    return jax.shard_map(
        on_device, mesh=mesh, in_specs=(spec,) * 5, out_specs=(spec,) * 5, check_vma=False
    )
```

```python
import functools
import math

import jax
import jax.numpy as jnp
from jax import lax
from jax.experimental import pallas as pl
from jax.experimental.pallas import tpu as pltpu
from jax.sharding import PartitionSpec as P

HD = 128
PAIR = 2
VMEM_BYTES = 60 << 20
UNIT, LANES, KEYS, WIDE = 4, 256, 128, 768
F32, BF16 = jnp.float32, jnp.bfloat16
NT = (((1,), (1,)), ((), ()))
TN = (((0,), (0,)), ((), ()))


def xor_permute(array, axis, size, mask):
    return lax.ppermute(array, axis, [(i, i ^ mask) for i in range(size)])


def attention_kernel(
    chips, tok, group, head, units, packing, layout, pos_ref, q_own, g_own, qg_rx, *refs
):
    n_in = len(packing)
    kv_in = refs[:n_in]
    dq_own, dq_oth = refs[n_in : n_in + 2]
    dkv_out = refs[n_in + 2 : n_in + 2 + len(layout)]
    qs, gs, kv, kt, acc, es, ds, ms, dqa, dqs, own_block, sent_blocks, sems, out_sems = refs[n_in + 2 + len(layout) :]
    span = PAIR * tok
    rows = UNIT * span
    width = group * HD
    chip, core = pos_ref[0], pos_ref[1]
    heads = q_own.shape[1] // (PAIR * width)
    col = pl.multiple_of((core * heads + head) * width, width)
    own = pl.multiple_of(core * tok, tok)
    oth = pl.multiple_of((1 - core) * tok, tok)
    copies = [
        (q_own.at[:, pl.ds(col, width)], qs.at[pl.ds(own, tok)]),
        (qg_rx.at[:, pl.ds(0, width)], qs.at[pl.ds(oth, tok)]),
        (g_own.at[:, pl.ds(col, width)], gs.at[pl.ds(own, tok)]),
        (qg_rx.at[:, pl.ds(width, width)], gs.at[pl.ds(oth, tok)]),
    ]
    for ref, (slots, lo) in zip(kv_in, packing):
        for i, s in enumerate(slots):
            copies.append((ref.at[pl.ds(i * span, span), pl.ds(lo, 2 * HD)], kv.at[chip ^ s]))
    started = [pltpu.make_async_copy(a, b, sems.at[i]) for i, (a, b) in enumerate(copies)]
    for c in started:
        c.start()
    acc[...] = jnp.zeros_like(acc)
    for c in started:
        c.wait()
    scale = 1.0 / math.sqrt(HD)
    log_scale = scale * math.log2(math.e)

    def turn(j, _):
        kt[j] = kv[j, :, :HD].T
        return 0

    lax.fori_loop(0, chip + 1, turn, 0)

    def columns_of(u):
        return pl.ds(pl.multiple_of(u * UNIT * HD, UNIT * HD), UNIT * HD)

    def stacked(ref, u):
        wide = ref[:, columns_of(u)]
        return jnp.concatenate([wide[:, i * HD : (i + 1) * HD] for i in range(UNIT)], 0)

    def unit(u, _):
        q = stacked(qs, u)
        g = stacked(gs, u)
        qt, gt = q.T, g.T

        def scores(j, carry, masked):
            out = []
            for t, lane in enumerate(range(0, rows, LANES)):
                top, total, weighted = carry[t]
                for i, key in enumerate(range(0, span, KEYS)):
                    s = lax.dot_general(
                        kv[j, key : key + KEYS, :HD],
                        q[lane : lane + LANES],
                        NT,
                        preferred_element_type=F32,
                    ) * log_scale
                    if masked:
                        key_ids = lax.broadcasted_iota(jnp.int32, s.shape, 0) + key
                        row_ids = lax.broadcasted_iota(jnp.int32, s.shape, 1) + lane % span
                        row_ids = jnp.where(row_ids >= span, row_ids - span, row_ids)
                        s = jnp.where(key_ids <= row_ids, s, -jnp.inf)
                    dp = lax.dot_general(
                        kv[j, key : key + KEYS, HD:],
                        g[lane : lane + LANES],
                        NT,
                        preferred_element_type=F32,
                    )
                    new = jnp.maximum(top, jnp.max(s, axis=0, keepdims=True))
                    e = jnp.exp2(s - new)
                    fade = jnp.exp2(top - new)
                    es[j, key : key + KEYS, lane : lane + LANES] = e
                    ds[j, key : key + KEYS, lane : lane + LANES] = dp
                    ms[j, i : i + 1, lane : lane + LANES] = new
                    total = total * fade + jnp.sum(e, axis=0, keepdims=True)
                    weighted = weighted * fade + jnp.sum(e * dp, axis=0, keepdims=True)
                    top = new
                out.append((top, total, weighted))
            return tuple(out)

        zero = jnp.zeros((1, LANES), F32)
        start = (jnp.full((1, LANES), -jnp.inf, F32), zero, zero)
        carry = scores(chip, (start,) * (rows // LANES), True)
        carry = lax.fori_loop(0, chip, lambda j, c: scores(j, c, False), carry)
        top, total, weighted = (jnp.concatenate(x, 1) for x in zip(*carry))
        inv = 1.0 / total
        delta = weighted * inv
        dqa[...] = jnp.zeros_like(dqa)

        def grads(j, _):
            for lane in range(0, rows, WIDE):
                at = slice(lane, lane + WIDE)
                ps, sgs = [], []
                for i, key in enumerate(range(0, span, KEYS)):
                    keys = slice(key, key + KEYS)
                    part = jnp.exp2(ms[j, i : i + 1, at] - top[:, at]) * inv[:, at]
                    p = es[j, keys, at] * part
                    ps.append(p.astype(BF16))
                    sgs.append((p * (ds[j, keys, at] - delta[:, at])).astype(BF16))
                p, sg = jnp.concatenate(ps, 0), jnp.concatenate(sgs, 0)
                acc[j, HD:] += lax.dot_general(gt[:, at], p, NT, preferred_element_type=F32)
                acc[j, :HD] += lax.dot_general(qt[:, at], sg, NT, preferred_element_type=F32)
                dqa[:, at] += jnp.dot(kt[j], sg, preferred_element_type=F32)
            return 0

        lax.fori_loop(0, chip + 1, grads, 0)
        out = (dqa[...] * scale).T.astype(BF16)
        dqs[:, columns_of(u)] = jnp.concatenate(
            [out[i * span : (i + 1) * span] for i in range(UNIT)], 1
        )
        for copy in query_copies(u):
            copy.start()
        return 0

    def query_copies(u):
        return [
            pltpu.make_async_copy(
                dqs.at[pl.ds(row, tok), columns_of(u)], ref.at[:, columns_of(u)], out_sems.at[i, u]
            )
            for i, (ref, row) in enumerate(((dq_own, own), (dq_oth, oth)))
        ]

    lax.fori_loop(0, units, unit, 0)
    leaving = [copy for u in range(units) for copy in query_copies(u)]
    starts, place = {(0,): 0}, 0
    for group_slots, _, _ in layout:
        if group_slots not in starts:
            starts[group_slots] = place
            place += len(group_slots) * span
    for n, (out, (group_slots, lo, hi)) in enumerate(zip(dkv_out, layout)):
        held = (own_block if group_slots == (0,) else sent_blocks).at[:, pl.ds(lo, hi - lo)]
        first_row = starts[group_slots]
        for i, s in enumerate(group_slots):
            j = chip ^ s
            part = pl.ds(first_row + i * span, span)

            @pl.when(j <= chip)
            def _():
                for half in range(lo, hi, HD):
                    cell = acc[j, half : half + HD]
                    cell = cell * scale if half == 0 else cell
                    held[part, half - lo : half - lo + HD] = cell.T.astype(held.dtype)

            @pl.when(j > chip)
            def _():
                held[part, :] = jnp.zeros((span, hi - lo), held.dtype)

        copy = pltpu.make_async_copy(
            held.at[pl.ds(first_row, len(group_slots) * span)], out, out_sems.at[2, n]
        )
        copy.start()
        leaving.append(copy)
    for copy in leaving:
        copy.wait()


def attention(pos, q_own, g_own, qg_rx, kv_parts, packing, head, direct):
    chips = sum(len(slots) for slots, _ in packing)
    width = qg_rx.shape[1] // 2
    tok = qg_rx.shape[0]
    span = PAIR * tok
    group = width // HD
    rows = UNIT * span
    if direct:
        layout = tuple(((s,), 0, 2 * HD) for s in range(chips))
    else:
        groups = [(0,)] + by_lowest_bit(chips)
        layout = tuple((slots, lo, lo + HD) for lo in (HD, 0) for slots in groups)
    hbm = pl.BlockSpec(memory_space=pltpu.HBM)
    out_shape = [jax.ShapeDtypeStruct((tok, width), BF16)] * 2 + [
        jax.ShapeDtypeStruct((len(slots) * span, hi - lo), F32 if slots == (0,) else BF16)
        for slots, lo, hi in layout
    ]
    inputs = [q_own, g_own, qg_rx, *kv_parts]
    outs = pl.pallas_call(
        functools.partial(
            attention_kernel, chips, tok, group, head, group // UNIT, packing, layout
        ),
        out_shape=out_shape,
        in_specs=[pl.BlockSpec(memory_space=pltpu.SMEM)] + [hbm] * len(inputs),
        out_specs=[hbm] * len(out_shape),
        scratch_shapes=[
            pltpu.VMEM((span, width), BF16),
            pltpu.VMEM((span, width), BF16),
            pltpu.VMEM((chips, span, 2 * HD), BF16),
            pltpu.VMEM((chips, HD, span), BF16),
            pltpu.VMEM((chips, 2 * HD, span), F32),
            pltpu.VMEM((chips, span, rows), F32),
            pltpu.VMEM((chips, span, rows), F32),
            pltpu.VMEM((chips, span // KEYS, rows), F32),
            pltpu.VMEM((HD, rows), F32),
            pltpu.VMEM((span, width), BF16),
            pltpu.VMEM((span, 2 * HD), F32),
            pltpu.VMEM(((chips - 1) * span, 2 * HD), BF16),
            pltpu.SemaphoreType.DMA((4 + chips,)),
            pltpu.SemaphoreType.DMA((3, max(len(layout), group // UNIT))),
        ],
        compiler_params=pltpu.CompilerParams(vmem_limit_bytes=VMEM_BYTES),
        cost_estimate=pl.CostEstimate(
            flops=400 * group * span * chips * span * HD, bytes_accessed=6 * span * width, transcendentals=0
        ),
        name="attention_grads",
    )(pos, *inputs)
    return outs


def product_kernel(chips, n_dp, tok, order, pos_ref, *refs):
    slots, halves, outs = refs[:n_dp], refs[n_dp : n_dp + PAIR], refs[n_dp + PAIR : -4]
    kvs, turned, held, sems = refs[-4:]
    depth = n_dp * tok
    block = held.shape[2]
    flat = [s for group in order for s in group]
    copies = []
    for i, s in enumerate(flat):
        columns = pl.ds(pl.multiple_of((pos_ref[0] ^ s) * block, block), block)
        for at, half in enumerate(halves):
            copy = pltpu.make_async_copy(
                half.at[:, columns], held.at[i, pl.ds(at * depth, depth)], sems.at[i, at]
            )
            copy.start()
            copies.append(copy)
    for s in range(n_dp):
        kvs[pos_ref[1] ^ s] = slots[s][...]
    for at in range(PAIR):
        rows = kvs[:, at * tok : (at + 1) * tok]
        turned[:, at * depth : (at + 1) * depth] = rows.reshape(depth, rows.shape[2]).T
    i = 0
    for out, group in zip(outs, order):
        for at in range(len(group)):
            for copy in copies[i * PAIR : (i + 1) * PAIR]:
                copy.wait()
            both = jnp.dot(turned[...], held[i], preferred_element_type=F32)
            out[at * block : (at + 1) * block] = both.T.astype(out.dtype)
            i += 1


def weight_products(pos, slots, hidden_own, hidden_oth, chips):
    n_dp = len(slots)
    span, wide = slots[0].shape
    depth, share = hidden_own.shape
    block = share // chips
    order = by_lowest_bit(chips) + [(0,)]
    vmem = pl.BlockSpec(memory_space=pltpu.VMEM)
    outs = pl.pallas_call(
        functools.partial(product_kernel, chips, n_dp, span // PAIR, order),
        in_specs=[pl.BlockSpec(memory_space=pltpu.SMEM)]
        + [vmem] * n_dp
        + [pl.BlockSpec(memory_space=pltpu.HBM)] * PAIR,
        out_specs=[pl.BlockSpec()] * len(order),
        out_shape=[
            jax.ShapeDtypeStruct((len(group) * block, wide), F32 if group == (0,) else BF16)
            for group in order
        ],
        scratch_shapes=[
            pltpu.VMEM((n_dp, span, wide), BF16),
            pltpu.VMEM((wide, PAIR * depth), BF16),
            pltpu.VMEM((chips, PAIR * depth, block), BF16),
            pltpu.SemaphoreType.DMA((chips, PAIR)),
        ],
        compiler_params=pltpu.CompilerParams(
            vmem_limit_bytes=VMEM_BYTES
        ),
        cost_estimate=pl.CostEstimate(flops=1, bytes_accessed=1, transcendentals=0),
        name="weight_products",
    )(pos, *slots, hidden_own, hidden_oth)
    return outs[-1], list(outs[:-1])


def by_lowest_bit(chips):
    bits = chips.bit_length() - 1
    return [tuple(s for s in range(1, chips) if s & -s == 1 << i) for i in range(bits)]


def on_device(queries, keys, values, out_grad, hidden):
    tok = queries.shape[0]
    n_dp, n_ctx = lax.axis_size("dp"), lax.axis_size("ctx")
    chips = n_ctx // PAIR
    kv_heads = keys.shape[1] // HD
    own_heads = kv_heads // PAIR
    width = queries.shape[1] // kv_heads
    dp, ctx = lax.axis_index("dp"), lax.axis_index("ctx")
    chip, core = ctx // PAIR, ctx % PAIR
    pos = jnp.stack([chip, core]).astype(jnp.int32)
    place = jnp.stack([chip, dp]).astype(jnp.int32)
    first = core == 0

    def swap(x):
        return xor_permute(x, "ctx", n_ctx, 1)

    def across(x, mask):
        return xor_permute(x, "ctx", n_ctx, mask * PAIR)

    def in_order(mine, theirs, axis):
        return jnp.where(
            first,
            jnp.concatenate([mine, theirs], axis),
            jnp.concatenate([theirs, mine], axis),
        )

    def columns(x, head, size):
        return lax.dynamic_slice_in_dim(x, head * size, size, 1)

    def after(x, *others):
        return lax.optimization_barrier((x, others))[0]

    def both_kv(owner):
        return jnp.concatenate(
            [columns(x, owner * own_heads + a, HD) for a in range(own_heads) for x in (keys, values)], 1
        )

    def rows_for_pair(a, queries, out_grad):
        theirs = (1 - core) * own_heads + a
        return jnp.concatenate([columns(queries, theirs, width), columns(out_grad, theirs, width)], 1)

    lowest = by_lowest_bit(chips)

    def own_first(total):
        return jnp.where(first, total, jnp.concatenate([total[tok:], total[:tok]], 0))

    def over_sequences(total):
        return [total] + [xor_permute(total, "dp", n_dp, s) for s in range(1, n_dp)]

    def product_blocks(slots, *gate):
        return weight_products(place, after(slots, *gate), hidden_own, hidden_oth, chips)

    def core_rows(summed):
        rows = share // n_ctx
        mine = lax.dynamic_slice_in_dim(summed, core * rows, rows, 0)
        theirs = lax.dynamic_slice_in_dim(summed, (1 - core) * rows, rows, 0)
        return mine, swap(theirs)

    def step(kept, groups, i, *gate):
        groups = list(groups)
        got = after(across(groups[i].astype(BF16), 1 << i), *gate)
        size = got.shape[0] // len(lowest[i])
        for at, s in enumerate(lowest[i]):
            piece = got[at * size : (at + 1) * size].astype(F32)
            to = s ^ (1 << i)
            if to == 0:
                kept = kept + piece
            else:
                g = next(g for g in range(len(lowest)) if to in lowest[g])
                at_to = lowest[g].index(to) * size
                pieces = [groups[g][:at_to], groups[g][at_to : at_to + size].astype(F32) + piece, groups[g][at_to + size :]]
                groups[g] = jnp.concatenate([x.astype(BF16) for x in pieces if x.shape[0]], 0)
        return kept, groups

    share = hidden.shape[1] // n_dp
    bits = len(lowest)

    kept, got = both_kv(core), swap(both_kv(1 - core))
    wide = 2 * HD
    kv_local = [in_order(kept[:, i * wide : (i + 1) * wide], got[:, i * wide : (i + 1) * wide], 0) for i in range(own_heads)]

    def doubling(slots, bits, *gate):
        for bit in bits:
            slots = slots | {s ^ bit: across(after(x, *gate), bit) for s, x in slots.items()}
        return slots

    far_first = [1 << i for i in reversed(range(bits))]
    queries_, out_grad_, hidden_ = after((queries, out_grad, hidden), kv_local)
    rx, rx1 = rows_for_pair(0, queries_, out_grad_), rows_for_pair(1, queries_, out_grad_)
    shares = hidden_.reshape(tok, n_dp, share).transpose(1, 0, 2)
    slots = doubling({0: kv_local[0]}, far_first[:-1])
    near = across(kv_local[0], 1)
    forward = {s: after(slots[s], rx, rx1, shares) for s in range(2, chips, 2)}
    slots |= {1: near} | {s ^ 1: across(x, 1) for s, x in forward.items()}
    rx, rx1 = swap(rx), swap(rx1)
    hidden_own = lax.all_to_all(shares, "dp", split_axis=0, concat_axis=0, tiled=True)
    hidden_own = hidden_own.reshape(n_dp * tok, share)
    parts = [slots[s] for s in range(chips)]
    packing = tuple(((s,), 0) for s in range(chips))
    local1 = after(kv_local[1], parts)
    parts1 = [local1] + [across(local1, s) for s in range(1, chips)]
    dq_own, dq_oth, *blocks = attention(
        pos, queries, out_grad, rx, parts, packing, 0, True
    )

    moved = [blocks[0]] + [across(blocks[s], s) for s in range(1, chips)]
    rx1, parts1 = after((rx1, parts1), blocks)
    dq_own1, dq_oth1, *blocks1 = attention(
        pos, queries, out_grad, rx1, parts1, packing, 1, False
    )
    one = sum(x.astype(F32) for x in after(moved, blocks1))
    hidden_own, dq_oth = after((hidden_own, dq_oth), one)
    hidden_oth = swap(hidden_own)

    total = own_first(one.astype(BF16))
    slots = over_sequences(total)
    size = 1 + len(lowest)
    value, key = ((blocks1[i], blocks1[i + 1 : i + size]) for i in (0, size))
    for i in range(bits - 1):
        value = step(*value, i)
        key = step(*key, i, value)
    product = product_blocks(slots, key)
    value = step(*value, bits - 1, product)
    total_v = own_first(value[0].astype(BF16))
    slots_v = over_sequences(total_v)
    key = step(*key, bits - 1, total_v)
    total_k = own_first(key[0].astype(BF16))
    slots_k = over_sequences(total_k)
    product_v = product_blocks(slots_v, total_k)
    for i in range(bits - 1):
        product = step(*product, i, product_v)
    product_k = product_blocks(slots_k, product)
    total, total_v, total_k, dq_oth, dq_oth1 = after(
        (total, total_v, total_k, dq_oth, dq_oth1), product_k[0]
    )
    for i in range(bits - 1):
        product_v = step(*product_v, i, product_k)
    product = step(*product, bits - 1, product_v)
    for i in range(bits - 1):
        product_k = step(*product_k, i, product)
    product_v = step(*product_v, bits - 1, product_k)
    product_k = step(*product_k, bits - 1, product_v)
    w_first, w_value, w_key = (core_rows(x[0]) for x in (product, product_v, product_k))
    both = swap(jnp.concatenate([total[tok:], total_k[tok:], total_v[tok:]], 1))
    wide = 2 * HD
    kv_first = total[:tok], both[:, :wide]
    kv_key = total_k[:tok], both[:, wide : wide + HD]
    kv_value = total_v[:tok], both[:, wide + HD :]

    def spread(one, two, lo):
        return in_order(*(jnp.concatenate([x[:, lo : lo + HD], y], 1) for x, y in zip(one, two)), 1)

    return (
        in_order(
            jnp.concatenate([dq_own, dq_own1], 1),
            swap(jnp.concatenate([dq_oth, dq_oth1], 1)),
            1,
        ),
        spread(kv_first, kv_key, 0),
        spread(kv_first, kv_value, HD),
        spread(w_first, w_key, 0),
        spread(w_first, w_value, HD),
    )


def solution(mesh):
    spec = P(("dp", "ctx"), None)
    return jax.shard_map(
        on_device, mesh=mesh, in_specs=(spec,) * 5, out_specs=(spec,) * 5, check_vma=False
    )
```

```python
import functools
import math

import jax
import jax.numpy as jnp
from jax import lax
from jax.experimental import pallas as pl
from jax.experimental.pallas import tpu as pltpu
from jax.sharding import PartitionSpec as P

HD = 128
PAIR = 2
VMEM_BYTES = 60 << 20
UNIT, LANES, KEYS, WIDE = 4, 256, 128, 768
F32, BF16 = jnp.float32, jnp.bfloat16
NT = (((1,), (1,)), ((), ()))
TN = (((0,), (0,)), ((), ()))


def xor_permute(array, axis, size, mask):
    return lax.ppermute(array, axis, [(i, i ^ mask) for i in range(size)])


def attention_kernel(
    chips, tok, group, head, units, packing, layout, pos_ref, q_own, g_own, qg_rx, *refs
):
    n_in = len(packing)
    kv_in = refs[:n_in]
    dq_own, dq_oth = refs[n_in : n_in + 2]
    dkv_out = refs[n_in + 2 : n_in + 2 + len(layout)]
    qs, gs, kv, kt, acc, es, ds, ms, dqa, dqs, own_block, sent_blocks, sems, out_sems = refs[n_in + 2 + len(layout) :]
    span = PAIR * tok
    rows = UNIT * span
    width = group * HD
    chip, core = pos_ref[0], pos_ref[1]
    heads = q_own.shape[1] // (PAIR * width)
    col = pl.multiple_of((core * heads + head) * width, width)
    own = pl.multiple_of(core * tok, tok)
    oth = pl.multiple_of((1 - core) * tok, tok)
    copies = [
        (q_own.at[:, pl.ds(col, width)], qs.at[pl.ds(own, tok)]),
        (qg_rx.at[:, pl.ds(0, width)], qs.at[pl.ds(oth, tok)]),
        (g_own.at[:, pl.ds(col, width)], gs.at[pl.ds(own, tok)]),
        (qg_rx.at[:, pl.ds(width, width)], gs.at[pl.ds(oth, tok)]),
    ]
    for ref, (slots, lo) in zip(kv_in, packing):
        for i, s in enumerate(slots):
            copies.append((ref.at[pl.ds(i * span, span), pl.ds(lo, 2 * HD)], kv.at[chip ^ s]))
    started = [pltpu.make_async_copy(a, b, sems.at[i]) for i, (a, b) in enumerate(copies)]
    for c in started:
        c.start()
    acc[...] = jnp.zeros_like(acc)
    for c in started:
        c.wait()
    scale = 1.0 / math.sqrt(HD)
    log_scale = scale * math.log2(math.e)

    def turn(j, _):
        kt[j] = kv[j, :, :HD].T
        return 0

    lax.fori_loop(0, chip + 1, turn, 0)

    def columns_of(u):
        return pl.ds(pl.multiple_of(u * UNIT * HD, UNIT * HD), UNIT * HD)

    def stacked(ref, u):
        wide = ref[:, columns_of(u)]
        return jnp.concatenate([wide[:, i * HD : (i + 1) * HD] for i in range(UNIT)], 0)

    def unit(u, _):
        q = stacked(qs, u)
        g = stacked(gs, u)
        qt, gt = q.T, g.T

        def scores(j, carry, masked):
            out = []
            for t, lane in enumerate(range(0, rows, LANES)):
                top, total, weighted = carry[t]
                for i, key in enumerate(range(0, span, KEYS)):
                    s = lax.dot_general(
                        kv[j, key : key + KEYS, :HD],
                        q[lane : lane + LANES],
                        NT,
                        preferred_element_type=F32,
                    ) * log_scale
                    if masked:
                        key_ids = lax.broadcasted_iota(jnp.int32, s.shape, 0) + key
                        row_ids = lax.broadcasted_iota(jnp.int32, s.shape, 1) + lane % span
                        row_ids = jnp.where(row_ids >= span, row_ids - span, row_ids)
                        s = jnp.where(key_ids <= row_ids, s, -jnp.inf)
                    dp = lax.dot_general(
                        kv[j, key : key + KEYS, HD:],
                        g[lane : lane + LANES],
                        NT,
                        preferred_element_type=F32,
                    )
                    new = jnp.maximum(top, jnp.max(s, axis=0, keepdims=True))
                    e = jnp.exp2(s - new)
                    fade = jnp.exp2(top - new)
                    es[j, key : key + KEYS, lane : lane + LANES] = e
                    ds[j, key : key + KEYS, lane : lane + LANES] = dp
                    ms[j, i : i + 1, lane : lane + LANES] = new
                    total = total * fade + jnp.sum(e, axis=0, keepdims=True)
                    weighted = weighted * fade + jnp.sum(e * dp, axis=0, keepdims=True)
                    top = new
                out.append((top, total, weighted))
            return tuple(out)

        zero = jnp.zeros((1, LANES), F32)
        start = (jnp.full((1, LANES), -jnp.inf, F32), zero, zero)
        carry = scores(chip, (start,) * (rows // LANES), True)
        carry = lax.fori_loop(0, chip, lambda j, c: scores(j, c, False), carry)
        top, total, weighted = (jnp.concatenate(x, 1) for x in zip(*carry))
        inv = 1.0 / total
        delta = weighted * inv
        dqa[...] = jnp.zeros_like(dqa)

        def grads(j, _):
            for lane in range(0, rows, WIDE):
                at = slice(lane, lane + WIDE)
                ps, sgs = [], []
                for i, key in enumerate(range(0, span, KEYS)):
                    keys = slice(key, key + KEYS)
                    part = jnp.exp2(ms[j, i : i + 1, at] - top[:, at]) * inv[:, at]
                    p = es[j, keys, at] * part
                    ps.append(p.astype(BF16))
                    sgs.append((p * (ds[j, keys, at] - delta[:, at])).astype(BF16))
                p, sg = jnp.concatenate(ps, 0), jnp.concatenate(sgs, 0)
                acc[j, HD:] += lax.dot_general(gt[:, at], p, NT, preferred_element_type=F32)
                acc[j, :HD] += lax.dot_general(qt[:, at], sg, NT, preferred_element_type=F32)
                dqa[:, at] += jnp.dot(kt[j], sg, preferred_element_type=F32)
            return 0

        lax.fori_loop(0, chip + 1, grads, 0)
        out = (dqa[...] * scale).T.astype(BF16)
        dqs[:, columns_of(u)] = jnp.concatenate(
            [out[i * span : (i + 1) * span] for i in range(UNIT)], 1
        )
        for copy in query_copies(u):
            copy.start()
        return 0

    def query_copies(u):
        return [
            pltpu.make_async_copy(
                dqs.at[pl.ds(row, tok), columns_of(u)], ref.at[:, columns_of(u)], out_sems.at[i, u]
            )
            for i, (ref, row) in enumerate(((dq_own, own), (dq_oth, oth)))
        ]

    lax.fori_loop(0, units, unit, 0)
    leaving = [copy for u in range(units) for copy in query_copies(u)]
    starts, place = {(0,): 0}, 0
    for group_slots, _, _ in layout:
        if group_slots not in starts:
            starts[group_slots] = place
            place += len(group_slots) * span
    for n, (out, (group_slots, lo, hi)) in enumerate(zip(dkv_out, layout)):
        held = (own_block if group_slots == (0,) else sent_blocks).at[:, pl.ds(lo, hi - lo)]
        first_row = starts[group_slots]
        for i, s in enumerate(group_slots):
            j = chip ^ s
            part = pl.ds(first_row + i * span, span)

            @pl.when(j <= chip)
            def _():
                for half in range(lo, hi, HD):
                    cell = acc[j, half : half + HD]
                    cell = cell * scale if half == 0 else cell
                    held[part, half - lo : half - lo + HD] = cell.T.astype(held.dtype)

            @pl.when(j > chip)
            def _():
                held[part, :] = jnp.zeros((span, hi - lo), held.dtype)

        copy = pltpu.make_async_copy(
            held.at[pl.ds(first_row, len(group_slots) * span)], out, out_sems.at[2, n]
        )
        copy.start()
        leaving.append(copy)
    for copy in leaving:
        copy.wait()


def attention(pos, q_own, g_own, qg_rx, kv_parts, packing, head, direct):
    chips = sum(len(slots) for slots, _ in packing)
    width = qg_rx.shape[1] // 2
    tok = qg_rx.shape[0]
    span = PAIR * tok
    group = width // HD
    rows = UNIT * span
    if direct:
        layout = tuple(((s,), 0, 2 * HD) for s in range(chips))
    else:
        groups = [(0,)] + by_lowest_bit(chips)
        layout = tuple((slots, lo, lo + HD) for lo in (HD, 0) for slots in groups)
    hbm = pl.BlockSpec(memory_space=pl.ANY)
    out_shape = [jax.ShapeDtypeStruct((tok, width), BF16)] * 2 + [
        jax.ShapeDtypeStruct((len(slots) * span, hi - lo), F32 if slots == (0,) else BF16)
        for slots, lo, hi in layout
    ]
    inputs = [q_own, g_own, qg_rx, *kv_parts]
    outs = pl.pallas_call(
        functools.partial(
            attention_kernel, chips, tok, group, head, group // UNIT, packing, layout
        ),
        out_shape=out_shape,
        in_specs=[pl.BlockSpec(memory_space=pltpu.SMEM)] + [hbm] * len(inputs),
        out_specs=[hbm] * len(out_shape),
        scratch_shapes=[
            pltpu.VMEM((span, width), BF16),
            pltpu.VMEM((span, width), BF16),
            pltpu.VMEM((chips, span, 2 * HD), BF16),
            pltpu.VMEM((chips, HD, span), BF16),
            pltpu.VMEM((chips, 2 * HD, span), F32),
            pltpu.VMEM((chips, span, rows), F32),
            pltpu.VMEM((chips, span, rows), F32),
            pltpu.VMEM((chips, span // KEYS, rows), F32),
            pltpu.VMEM((HD, rows), F32),
            pltpu.VMEM((span, width), BF16),
            pltpu.VMEM((span, 2 * HD), F32),
            pltpu.VMEM(((chips - 1) * span, 2 * HD), BF16),
            pltpu.SemaphoreType.DMA((4 + chips,)),
            pltpu.SemaphoreType.DMA((3, max(len(layout), group // UNIT))),
        ],
        compiler_params=pltpu.CompilerParams(vmem_limit_bytes=VMEM_BYTES),
        cost_estimate=pl.CostEstimate(
            flops=400 * group * span * chips * span * HD, bytes_accessed=6 * span * width, transcendentals=0
        ),
        name="attention_grads",
    )(pos, *inputs)
    return outs


def product_kernel(chips, n_dp, tok, order, pos_ref, *refs):
    slots, halves, outs = refs[:n_dp], refs[n_dp : n_dp + PAIR], refs[n_dp + PAIR : -5]
    kvs, turned, *staged, out_sems = refs[-5:]
    depth = n_dp * tok
    block = staged[1].shape[0]
    flat = [s for group in order for s in group]
    for s in range(n_dp):
        kvs[pos_ref[2] ^ s] = slots[s][...]
    for at in range(PAIR):
        rows = kvs[:, at * tok : (at + 1) * tok]
        turned[at] = rows.reshape(depth, rows.shape[2]).T
    leaving = []
    for i, s in enumerate(flat):
        columns = pl.ds(pl.multiple_of((pos_ref[0] ^ s) * block, block), block)
        both = sum(
            jnp.dot(turned[at], halves[at][:, columns], preferred_element_type=F32)
            for at in range(PAIR)
        ).T
        n = next(n for n, group in enumerate(order) if s in group)
        target = outs[n].at[pl.ds(order[n].index(s) * block, block)]
        if s == 0:
            staged[1][...] = both
            source = staged[1]
        else:
            staged[0][i] = both.astype(BF16)
            source = staged[0].at[i]
        copy = pltpu.make_async_copy(source, target, out_sems.at[i])
        copy.start()
        leaving.append(copy)
    for copy in leaving:
        copy.wait()


def weight_products(pos, slots, hidden_own, hidden_oth, chips):
    n_dp = len(slots)
    span, wide = slots[0].shape
    depth, share = hidden_own.shape
    block = share // chips
    order = by_lowest_bit(chips) + [(0,)]
    anywhere = pl.BlockSpec(memory_space=pl.ANY)
    outs = pl.pallas_call(
        functools.partial(product_kernel, chips, n_dp, span // PAIR, order),
        in_specs=[pl.BlockSpec(memory_space=pltpu.SMEM)] + [pl.BlockSpec(memory_space=pltpu.VMEM)] * (n_dp + PAIR),
        out_specs=[anywhere] * len(order),
        out_shape=[
            jax.ShapeDtypeStruct((len(group) * block, wide), F32 if group == (0,) else BF16)
            for group in order
        ],
        scratch_shapes=[
            pltpu.VMEM((n_dp, span, wide), BF16),
            pltpu.VMEM((PAIR, wide, depth), BF16),
            pltpu.VMEM((chips - 1, block, wide), BF16),
            pltpu.VMEM((block, wide), F32),
            pltpu.SemaphoreType.DMA((chips,)),
        ],
        compiler_params=pltpu.CompilerParams(vmem_limit_bytes=16 << 20),
        cost_estimate=pl.CostEstimate(flops=1, bytes_accessed=1, transcendentals=0),
        name="weight_products",
    )(pos, *slots, hidden_own, hidden_oth)
    return outs[-1], list(outs[:-1])


def by_lowest_bit(chips):
    bits = chips.bit_length() - 1
    return [tuple(s for s in range(1, chips) if s & -s == 1 << i) for i in range(bits)]


def on_device(queries, keys, values, out_grad, hidden):
    tok = queries.shape[0]
    n_dp, n_ctx = lax.axis_size("dp"), lax.axis_size("ctx")
    chips = n_ctx // PAIR
    kv_heads = keys.shape[1] // HD
    own_heads = kv_heads // PAIR
    width = queries.shape[1] // kv_heads
    dp, ctx = lax.axis_index("dp"), lax.axis_index("ctx")
    chip, core = ctx // PAIR, ctx % PAIR
    pos = jnp.stack([chip, core, dp]).astype(jnp.int32)
    first = core == 0

    def swap(x):
        return xor_permute(x, "ctx", n_ctx, 1)

    def across(x, mask):
        return xor_permute(x, "ctx", n_ctx, mask * PAIR)

    def in_order(mine, theirs, axis):
        return jnp.where(
            first,
            jnp.concatenate([mine, theirs], axis),
            jnp.concatenate([theirs, mine], axis),
        )

    def columns(x, head, size):
        return lax.dynamic_slice_in_dim(x, head * size, size, 1)

    def after(x, *others):
        return lax.optimization_barrier((x, others))[0]

    def both_kv(owner):
        return jnp.concatenate(
            [columns(x, owner * own_heads + a, HD) for a in range(own_heads) for x in (keys, values)], 1
        )

    def rows_for_pair(a, queries, out_grad):
        theirs = (1 - core) * own_heads + a
        return jnp.concatenate([columns(queries, theirs, width), columns(out_grad, theirs, width)], 1)

    lowest = by_lowest_bit(chips)

    def own_first(total):
        return jnp.where(first, total, jnp.concatenate([total[tok:], total[:tok]], 0))

    def over_sequences(total):
        return [total] + [xor_permute(total, "dp", n_dp, s) for s in range(1, n_dp)]

    def product_blocks(slots, *gate):
        return weight_products(pos, after(slots, *gate), hidden_own, hidden_oth, chips)

    def core_rows(summed):
        rows = share // n_ctx
        mine = lax.dynamic_slice_in_dim(summed, core * rows, rows, 0)
        theirs = lax.dynamic_slice_in_dim(summed, (1 - core) * rows, rows, 0)
        return mine, swap(theirs)

    def step(kept, groups, i, *gate):
        groups = list(groups)
        got = after(across(groups[i].astype(BF16), 1 << i), *gate)
        size = got.shape[0] // len(lowest[i])
        for at, s in enumerate(lowest[i]):
            piece = got[at * size : (at + 1) * size].astype(F32)
            to = s ^ (1 << i)
            if to == 0:
                kept = kept + piece
            else:
                g = next(g for g in range(len(lowest)) if to in lowest[g])
                at_to = lowest[g].index(to) * size
                pieces = [groups[g][:at_to], groups[g][at_to : at_to + size].astype(F32) + piece, groups[g][at_to + size :]]
                groups[g] = jnp.concatenate([x.astype(BF16) for x in pieces if x.shape[0]], 0)
        return kept, groups

    share = hidden.shape[1] // n_dp
    bits = len(lowest)

    kept, got = both_kv(core), swap(both_kv(1 - core))
    wide = 2 * HD
    kv_local = [in_order(kept[:, i * wide : (i + 1) * wide], got[:, i * wide : (i + 1) * wide], 0) for i in range(own_heads)]

    def doubling(slots, bits, *gate):
        for bit in bits:
            slots = slots | {s ^ bit: across(after(x, *gate), bit) for s, x in slots.items()}
        return slots

    far_first = [1 << i for i in reversed(range(bits))]
    queries_, out_grad_, hidden_ = after((queries, out_grad, hidden), kv_local)
    rx, rx1 = rows_for_pair(0, queries_, out_grad_), rows_for_pair(1, queries_, out_grad_)
    shares = hidden_.reshape(tok, n_dp, share).transpose(1, 0, 2)
    slots = doubling({0: kv_local[0]}, far_first[:-1])
    near = across(kv_local[0], 1)
    forward = {s: after(slots[s], rx, rx1, shares) for s in range(2, chips, 2)}
    slots |= {1: near} | {s ^ 1: across(x, 1) for s, x in forward.items()}
    rx, rx1 = swap(rx), swap(rx1)
    hidden_own = lax.all_to_all(shares, "dp", split_axis=0, concat_axis=0, tiled=True)
    hidden_own = hidden_own.reshape(n_dp * tok, share)
    parts = [slots[s] for s in range(chips)]
    packing = tuple(((s,), 0) for s in range(chips))
    local1 = after(kv_local[1], parts)
    parts1 = [local1] + [across(local1, s) for s in range(1, chips)]
    dq_own, dq_oth, *blocks = attention(
        pos, queries, out_grad, rx, parts, packing, 0, True
    )

    moved = [blocks[0]] + [across(blocks[s], s) for s in range(1, chips)]
    rx1, parts1 = after((rx1, parts1), blocks)
    dq_own1, dq_oth1, *blocks1 = attention(
        pos, queries, out_grad, rx1, parts1, packing, 1, False
    )
    one = sum(x.astype(F32) for x in after(moved, blocks1))
    hidden_own, dq_oth = after((hidden_own, dq_oth), one)
    hidden_oth = swap(hidden_own)

    total = own_first(one.astype(BF16))
    slots = over_sequences(total)
    size = 1 + len(lowest)
    value, key = ((blocks1[i], blocks1[i + 1 : i + size]) for i in (0, size))
    for i in range(bits - 1):
        value = step(*value, i)
        key = step(*key, i, value)
    product = product_blocks(slots, key)
    value = step(*value, bits - 1, product)
    total_v = own_first(value[0].astype(BF16))
    slots_v = over_sequences(total_v)
    key = step(*key, bits - 1, total_v)
    total_k = own_first(key[0].astype(BF16))
    slots_k = over_sequences(total_k)
    product_v = product_blocks(slots_v, total_k)
    for i in range(bits - 1):
        product = step(*product, i, product_v)
    product_k = product_blocks(slots_k, product)
    total, total_v, total_k, dq_oth, dq_oth1 = after(
        (total, total_v, total_k, dq_oth, dq_oth1), product_k[0]
    )
    for i in range(bits - 1):
        product_v = step(*product_v, i, product_k)
    product = step(*product, bits - 1, product_v)
    for i in range(bits - 1):
        product_k = step(*product_k, i, product)
    product_v = step(*product_v, bits - 1, product_k)

    def spread(one, two, lo):
        return in_order(*(jnp.concatenate([x[:, lo : lo + HD], y], 1) for x, y in zip(one, two)), 1)

    both = swap(jnp.concatenate([total[tok:], total_k[tok:], total_v[tok:]], 1))
    wide = 2 * HD
    kv_first = total[:tok], both[:, :wide]
    w_first, w_value = core_rows(product[0]), core_rows(product_v[0])
    done = (
        in_order(
            jnp.concatenate([dq_own, dq_own1], 1),
            swap(jnp.concatenate([dq_oth, dq_oth1], 1)),
            1,
        ),
        spread(kv_first, (total_k[:tok], both[:, wide : wide + HD]), 0),
        spread(kv_first, (total_v[:tok], both[:, wide + HD :]), HD),
    )
    value_weights = spread(w_first, w_value, HD)
    product_k = step(*product_k, bits - 1, done, value_weights)
    return *done, spread(w_first, core_rows(product_k[0]), 0), value_weights


def solution(mesh):
    spec = P(("dp", "ctx"), None)
    return jax.shard_map(
        on_device, mesh=mesh, in_specs=(spec,) * 5, out_specs=(spec,) * 5, check_vma=False
    )
```

```python
import functools
import math

import jax
import jax.numpy as jnp
from jax import lax
from jax.experimental import pallas as pl
from jax.experimental.pallas import tpu as pltpu
from jax.sharding import PartitionSpec as P

HD = 128
PAIR = 2
VMEM_BYTES = 60 << 20
UNIT, LANES, KEYS, WIDE = 4, 256, 128, 768
F32, BF16 = jnp.float32, jnp.bfloat16
NT = (((1,), (1,)), ((), ()))
TN = (((0,), (0,)), ((), ()))


def xor_permute(array, axis, size, mask):
    return lax.ppermute(array, axis, [(i, i ^ mask) for i in range(size)])


def attention_kernel(
    chips, tok, group, head, units, packing, layout, pos_ref, q_own, g_own, qg_rx, *refs
):
    n_in = len(packing)
    kv_in = refs[:n_in]
    dq_own, dq_oth = refs[n_in : n_in + 2]
    dkv_out = refs[n_in + 2 : n_in + 2 + len(layout)]
    qs, gs, kv, kt, acc, es, ds, ms, dqa, dqs, own_block, sent_blocks, sems, out_sems = refs[n_in + 2 + len(layout) :]
    span = PAIR * tok
    rows = UNIT * span
    width = group * HD
    chip, core = pos_ref[0], pos_ref[1]
    heads = q_own.shape[1] // (PAIR * width)
    col = pl.multiple_of((core * heads + head) * width, width)
    own = pl.multiple_of(core * tok, tok)
    oth = pl.multiple_of((1 - core) * tok, tok)
    copies = [
        (q_own.at[:, pl.ds(col, width)], qs.at[pl.ds(own, tok)]),
        (qg_rx.at[:, pl.ds(0, width)], qs.at[pl.ds(oth, tok)]),
        (g_own.at[:, pl.ds(col, width)], gs.at[pl.ds(own, tok)]),
        (qg_rx.at[:, pl.ds(width, width)], gs.at[pl.ds(oth, tok)]),
    ]
    for ref, (slots, lo) in zip(kv_in, packing):
        for i, s in enumerate(slots):
            copies.append((ref.at[pl.ds(i * span, span), pl.ds(lo, 2 * HD)], kv.at[chip ^ s]))
    started = [pltpu.make_async_copy(a, b, sems.at[i]) for i, (a, b) in enumerate(copies)]
    for c in started:
        c.start()
    acc[...] = jnp.zeros_like(acc)
    for c in started:
        c.wait()
    scale = 1.0 / math.sqrt(HD)
    log_scale = scale * math.log2(math.e)

    def turn(j, _):
        kt[j] = kv[j, :, :HD].T
        return 0

    lax.fori_loop(0, chip + 1, turn, 0)

    def columns_of(u):
        return pl.ds(pl.multiple_of(u * UNIT * HD, UNIT * HD), UNIT * HD)

    def stacked(ref, u):
        wide = ref[:, columns_of(u)]
        return jnp.concatenate([wide[:, i * HD : (i + 1) * HD] for i in range(UNIT)], 0)

    def unit(u, _):
        q = stacked(qs, u)
        g = stacked(gs, u)
        qt, gt = q.T, g.T

        def scores(j, carry, masked):
            out = []
            for t, lane in enumerate(range(0, rows, LANES)):
                top, total, weighted = carry[t]
                for i, key in enumerate(range(0, span, KEYS)):
                    s = lax.dot_general(
                        kv[j, key : key + KEYS, :HD],
                        q[lane : lane + LANES],
                        NT,
                        preferred_element_type=F32,
                    ) * log_scale
                    if masked:
                        key_ids = lax.broadcasted_iota(jnp.int32, s.shape, 0) + key
                        row_ids = lax.broadcasted_iota(jnp.int32, s.shape, 1) + lane % span
                        row_ids = jnp.where(row_ids >= span, row_ids - span, row_ids)
                        s = jnp.where(key_ids <= row_ids, s, -jnp.inf)
                    dp = lax.dot_general(
                        kv[j, key : key + KEYS, HD:],
                        g[lane : lane + LANES],
                        NT,
                        preferred_element_type=F32,
                    )
                    new = jnp.maximum(top, jnp.max(s, axis=0, keepdims=True))
                    e = jnp.exp2(s - new)
                    fade = jnp.exp2(top - new)
                    es[j, key : key + KEYS, lane : lane + LANES] = e
                    ds[j, key : key + KEYS, lane : lane + LANES] = dp
                    ms[j, i : i + 1, lane : lane + LANES] = new
                    total = total * fade + jnp.sum(e, axis=0, keepdims=True)
                    weighted = weighted * fade + jnp.sum(e * dp, axis=0, keepdims=True)
                    top = new
                out.append((top, total, weighted))
            return tuple(out)

        zero = jnp.zeros((1, LANES), F32)
        start = (jnp.full((1, LANES), -jnp.inf, F32), zero, zero)
        carry = scores(chip, (start,) * (rows // LANES), True)
        carry = lax.fori_loop(0, chip, lambda j, c: scores(j, c, False), carry)
        top, total, weighted = (jnp.concatenate(x, 1) for x in zip(*carry))
        inv = 1.0 / total
        delta = weighted * inv
        dqa[...] = jnp.zeros_like(dqa)

        def grads(j, _):
            for lane in range(0, rows, WIDE):
                at = slice(lane, lane + WIDE)
                ps, sgs = [], []
                for i, key in enumerate(range(0, span, KEYS)):
                    keys = slice(key, key + KEYS)
                    part = jnp.exp2(ms[j, i : i + 1, at] - top[:, at]) * inv[:, at]
                    p = es[j, keys, at] * part
                    ps.append(p.astype(BF16))
                    sgs.append((p * (ds[j, keys, at] - delta[:, at])).astype(BF16))
                p, sg = jnp.concatenate(ps, 0), jnp.concatenate(sgs, 0)
                acc[j, HD:] += lax.dot_general(gt[:, at], p, NT, preferred_element_type=F32)
                acc[j, :HD] += lax.dot_general(qt[:, at], sg, NT, preferred_element_type=F32)
                dqa[:, at] += jnp.dot(kt[j], sg, preferred_element_type=F32)
            return 0

        lax.fori_loop(0, chip + 1, grads, 0)
        out = (dqa[...] * scale).T.astype(BF16)
        dqs[:, columns_of(u)] = jnp.concatenate(
            [out[i * span : (i + 1) * span] for i in range(UNIT)], 1
        )
        for copy in query_copies(u):
            copy.start()
        return 0

    def query_copies(u):
        return [
            pltpu.make_async_copy(
                dqs.at[pl.ds(row, tok), columns_of(u)], ref.at[:, columns_of(u)], out_sems.at[i, u]
            )
            for i, (ref, row) in enumerate(((dq_own, own), (dq_oth, oth)))
        ]

    lax.fori_loop(0, units, unit, 0)
    leaving = [copy for u in range(units) for copy in query_copies(u)]
    starts, place = {(0,): 0}, 0
    for group_slots, _, _ in layout:
        if group_slots not in starts:
            starts[group_slots] = place
            place += len(group_slots) * span
    for n, (out, (group_slots, lo, hi)) in enumerate(zip(dkv_out, layout)):
        held = (own_block if group_slots == (0,) else sent_blocks).at[:, pl.ds(lo, hi - lo)]
        first_row = starts[group_slots]
        for i, s in enumerate(group_slots):
            j = chip ^ s
            part = pl.ds(first_row + i * span, span)

            @pl.when(j <= chip)
            def _():
                for half in range(lo, hi, HD):
                    cell = acc[j, half : half + HD]
                    cell = cell * scale if half == 0 else cell
                    held[part, half - lo : half - lo + HD] = cell.T.astype(held.dtype)

            @pl.when(j > chip)
            def _():
                held[part, :] = jnp.zeros((span, hi - lo), held.dtype)

        copy = pltpu.make_async_copy(
            held.at[pl.ds(first_row, len(group_slots) * span)], out, out_sems.at[2, n]
        )
        copy.start()
        leaving.append(copy)
    for copy in leaving:
        copy.wait()


def attention(pos, q_own, g_own, qg_rx, kv_parts, packing, head, direct):
    chips = sum(len(slots) for slots, _ in packing)
    width = qg_rx.shape[1] // 2
    tok = qg_rx.shape[0]
    span = PAIR * tok
    group = width // HD
    rows = UNIT * span
    if direct:
        layout = tuple(((s,), 0, 2 * HD) for s in range(chips))
    else:
        groups = [(0,)] + by_lowest_bit(chips)
        layout = tuple((slots, lo, lo + HD) for lo in (HD, 0) for slots in groups)
    hbm = pl.BlockSpec(memory_space=pl.ANY)
    out_shape = [jax.ShapeDtypeStruct((tok, width), BF16)] * 2 + [
        jax.ShapeDtypeStruct((len(slots) * span, hi - lo), F32 if slots == (0,) else BF16)
        for slots, lo, hi in layout
    ]
    inputs = [q_own, g_own, qg_rx, *kv_parts]
    outs = pl.pallas_call(
        functools.partial(
            attention_kernel, chips, tok, group, head, group // UNIT, packing, layout
        ),
        out_shape=out_shape,
        in_specs=[pl.BlockSpec(memory_space=pltpu.SMEM)] + [hbm] * len(inputs),
        out_specs=[hbm] * len(out_shape),
        scratch_shapes=[
            pltpu.VMEM((span, width), BF16),
            pltpu.VMEM((span, width), BF16),
            pltpu.VMEM((chips, span, 2 * HD), BF16),
            pltpu.VMEM((chips, HD, span), BF16),
            pltpu.VMEM((chips, 2 * HD, span), F32),
            pltpu.VMEM((chips, span, rows), F32),
            pltpu.VMEM((chips, span, rows), F32),
            pltpu.VMEM((chips, span // KEYS, rows), F32),
            pltpu.VMEM((HD, rows), F32),
            pltpu.VMEM((span, width), BF16),
            pltpu.VMEM((span, 2 * HD), F32),
            pltpu.VMEM(((chips - 1) * span, 2 * HD), BF16),
            pltpu.SemaphoreType.DMA((4 + chips,)),
            pltpu.SemaphoreType.DMA((3, max(len(layout), group // UNIT))),
        ],
        compiler_params=pltpu.CompilerParams(vmem_limit_bytes=VMEM_BYTES),
        cost_estimate=pl.CostEstimate(
            flops=400 * group * span * chips * span * HD, bytes_accessed=6 * span * width, transcendentals=0
        ),
        name="attention_grads",
    )(pos, *inputs)
    return outs


def product_kernel(chips, n_dp, tok, order, pos_ref, *refs):
    slots, halves, outs = refs[:n_dp], refs[n_dp : n_dp + PAIR], refs[n_dp + PAIR : -5]
    kvs, turned, *staged, out_sems = refs[-5:]
    depth = n_dp * tok
    block = staged[1].shape[0]
    flat = [s for group in order for s in group]
    for s in range(n_dp):
        kvs[pos_ref[2] ^ s] = slots[s][...]
    for at in range(PAIR):
        rows = kvs[:, at * tok : (at + 1) * tok]
        turned[at] = rows.reshape(depth, rows.shape[2]).T
    leaving = []
    for i, s in enumerate(flat):
        columns = pl.ds(pl.multiple_of((pos_ref[0] ^ s) * block, block), block)
        both = sum(
            jnp.dot(turned[at], halves[at][:, columns], preferred_element_type=F32)
            for at in range(PAIR)
        ).T
        n = next(n for n, group in enumerate(order) if s in group)
        target = outs[n].at[pl.ds(order[n].index(s) * block, block)]
        if s == 0:
            staged[1][...] = both
            source = staged[1]
        else:
            staged[0][i] = both.astype(BF16)
            source = staged[0].at[i]
        copy = pltpu.make_async_copy(source, target, out_sems.at[i])
        copy.start()
        leaving.append(copy)
    for copy in leaving:
        copy.wait()


def weight_products(pos, slots, hidden_own, hidden_oth, chips):
    n_dp = len(slots)
    span, wide = slots[0].shape
    depth, share = hidden_own.shape
    block = share // chips
    order = by_lowest_bit(chips) + [(0,)]
    anywhere = pl.BlockSpec(memory_space=pl.ANY)
    outs = pl.pallas_call(
        functools.partial(product_kernel, chips, n_dp, span // PAIR, order),
        in_specs=[pl.BlockSpec(memory_space=pltpu.SMEM)] + [pl.BlockSpec(memory_space=pltpu.VMEM)] * (n_dp + PAIR),
        out_specs=[anywhere] * len(order),
        out_shape=[
            jax.ShapeDtypeStruct((len(group) * block, wide), F32 if group == (0,) else BF16)
            for group in order
        ],
        scratch_shapes=[
            pltpu.VMEM((n_dp, span, wide), BF16),
            pltpu.VMEM((PAIR, wide, depth), BF16),
            pltpu.VMEM((chips - 1, block, wide), BF16),
            pltpu.VMEM((block, wide), F32),
            pltpu.SemaphoreType.DMA((chips,)),
        ],
        compiler_params=pltpu.CompilerParams(vmem_limit_bytes=16 << 20),
        cost_estimate=pl.CostEstimate(flops=1, bytes_accessed=1, transcendentals=0),
        name="weight_products",
    )(pos, *slots, hidden_own, hidden_oth)
    return outs[-1], list(outs[:-1])


def by_lowest_bit(chips):
    bits = chips.bit_length() - 1
    return [tuple(s for s in range(1, chips) if s & -s == 1 << i) for i in range(bits)]


def on_device(queries, keys, values, out_grad, hidden):
    tok = queries.shape[0]
    n_dp, n_ctx = lax.axis_size("dp"), lax.axis_size("ctx")
    chips = n_ctx // PAIR
    kv_heads = keys.shape[1] // HD
    own_heads = kv_heads // PAIR
    width = queries.shape[1] // kv_heads
    dp, ctx = lax.axis_index("dp"), lax.axis_index("ctx")
    chip, core = ctx // PAIR, ctx % PAIR
    pos = jnp.stack([chip, core, dp]).astype(jnp.int32)
    first = core == 0

    def swap(x):
        return xor_permute(x, "ctx", n_ctx, 1)

    def across(x, mask):
        return xor_permute(x, "ctx", n_ctx, mask * PAIR)

    def in_order(mine, theirs, axis):
        return jnp.where(
            first,
            jnp.concatenate([mine, theirs], axis),
            jnp.concatenate([theirs, mine], axis),
        )

    def columns(x, head, size):
        return lax.dynamic_slice_in_dim(x, head * size, size, 1)

    def after(x, *others):
        return lax.optimization_barrier((x, others))[0]

    def both_kv(owner):
        return jnp.concatenate(
            [columns(x, owner * own_heads + a, HD) for a in range(own_heads) for x in (keys, values)], 1
        )

    def rows_for_pair(a, queries, out_grad):
        theirs = (1 - core) * own_heads + a
        return jnp.concatenate([columns(queries, theirs, width), columns(out_grad, theirs, width)], 1)

    lowest = by_lowest_bit(chips)

    def own_first(total):
        return jnp.where(first, total, jnp.concatenate([total[tok:], total[:tok]], 0))

    def over_sequences(total):
        return [total] + [xor_permute(total, "dp", n_dp, s) for s in range(1, n_dp)]

    def product_blocks(slots, *gate):
        return weight_products(pos, after(slots, *gate), hidden_own, hidden_oth, chips)

    def core_rows(summed):
        rows = share // n_ctx
        mine = lax.dynamic_slice_in_dim(summed, core * rows, rows, 0)
        theirs = lax.dynamic_slice_in_dim(summed, (1 - core) * rows, rows, 0)
        return mine, swap(theirs)

    def step(kept, groups, i, *gate):
        groups = list(groups)
        got = after(across(groups[i].astype(BF16), 1 << i), *gate)
        size = got.shape[0] // len(lowest[i])
        for at, s in enumerate(lowest[i]):
            piece = got[at * size : (at + 1) * size].astype(F32)
            to = s ^ (1 << i)
            if to == 0:
                kept = kept + piece
            else:
                g = next(g for g in range(len(lowest)) if to in lowest[g])
                at_to = lowest[g].index(to) * size
                pieces = [groups[g][:at_to], groups[g][at_to : at_to + size].astype(F32) + piece, groups[g][at_to + size :]]
                groups[g] = jnp.concatenate([x.astype(BF16) for x in pieces if x.shape[0]], 0)
        return kept, groups

    share = hidden.shape[1] // n_dp
    bits = len(lowest)

    kept, got = both_kv(core), swap(both_kv(1 - core))
    wide = 2 * HD
    kv_local = [in_order(kept[:, i * wide : (i + 1) * wide], got[:, i * wide : (i + 1) * wide], 0) for i in range(own_heads)]

    def doubling(slots, bits, *gate):
        for bit in bits:
            slots = slots | {s ^ bit: across(after(x, *gate), bit) for s, x in slots.items()}
        return slots

    far_first = [1 << i for i in reversed(range(bits))]
    queries_, out_grad_, hidden_ = after((queries, out_grad, hidden), kv_local)
    rx, rx1 = rows_for_pair(0, queries_, out_grad_), rows_for_pair(1, queries_, out_grad_)
    shares = hidden_.reshape(tok, n_dp, share).transpose(1, 0, 2)
    slots = doubling({0: kv_local[0]}, far_first[:-1])
    near = across(kv_local[0], 1)
    forward = {s: after(slots[s], rx, shares) for s in range(2, chips, 2)}
    slots |= {1: near} | {s ^ 1: across(x, 1) for s, x in forward.items()}
    rx, rx1 = swap(rx), swap(rx1)
    hidden_own = lax.all_to_all(shares, "dp", split_axis=0, concat_axis=0, tiled=True)
    hidden_own = hidden_own.reshape(n_dp * tok, share)
    parts = [slots[s] for s in range(chips)]
    packing = tuple(((s,), 0) for s in range(chips))
    local1 = after(kv_local[1], parts)
    parts1 = [local1] + [across(local1, s) for s in range(1, chips)]
    dq_own, dq_oth, *blocks = attention(
        pos, queries, out_grad, rx, parts, packing, 0, True
    )

    moved = [blocks[0]] + [across(blocks[s], s) for s in range(1, chips)]
    rx1, parts1, hidden_own = after((rx1, parts1, hidden_own), blocks)
    hidden_oth = swap(hidden_own)
    dq_own1, dq_oth1, *blocks1 = attention(
        pos, queries, out_grad, rx1, parts1, packing, 1, False
    )
    one = sum(x.astype(F32) for x in after(moved, blocks1))
    hidden_oth, dq_oth = after((hidden_oth, dq_oth), one)

    total = own_first(one.astype(BF16))
    slots = over_sequences(total)
    size = 1 + len(lowest)
    value, key = ((blocks1[i], blocks1[i + 1 : i + size]) for i in (0, size))
    for i in range(bits - 1):
        value = step(*value, i)
        key = step(*key, i, value)
    product = product_blocks(slots, key)
    value = step(*value, bits - 1, product)
    total_v = own_first(value[0].astype(BF16))
    slots_v = over_sequences(total_v)
    key = step(*key, bits - 1, total_v)
    total_k = own_first(key[0].astype(BF16))
    slots_k = over_sequences(total_k)
    product_v = product_blocks(slots_v, total_k)
    for i in range(bits - 1):
        product = step(*product, i, product_v)
    product_k = product_blocks(slots_k, product)
    total, total_v, total_k, dq_oth, dq_oth1 = after(
        (total, total_v, total_k, dq_oth, dq_oth1), product_k[0]
    )
    for i in range(bits - 1):
        product_v = step(*product_v, i, product_k)
    for i in range(bits - 1):
        product_k = step(*product_k, i, product_v)
    product = step(*product, bits - 1, product_k)
    product_v = step(*product_v, bits - 1, product)

    def spread(one, two, lo):
        return in_order(*(jnp.concatenate([x[:, lo : lo + HD], y], 1) for x, y in zip(one, two)), 1)

    both = swap(jnp.concatenate([total[tok:], total_k[tok:], total_v[tok:]], 1))
    wide = 2 * HD
    kv_first = total[:tok], both[:, :wide]
    w_first, w_value = core_rows(product[0]), core_rows(product_v[0])
    done = (
        in_order(
            jnp.concatenate([dq_own, dq_own1], 1),
            swap(jnp.concatenate([dq_oth, dq_oth1], 1)),
            1,
        ),
        spread(kv_first, (total_k[:tok], both[:, wide : wide + HD]), 0),
        spread(kv_first, (total_v[:tok], both[:, wide + HD :]), HD),
    )
    value_weights = spread(w_first, w_value, HD)
    product_k = step(*product_k, bits - 1, done, value_weights)
    return *done, spread(w_first, core_rows(product_k[0]), 0), value_weights


def solution(mesh):
    spec = P(("dp", "ctx"), None)
    return jax.shard_map(
        on_device, mesh=mesh, in_specs=(spec,) * 5, out_specs=(spec,) * 5, check_vma=False
    )
```

```python
import functools
import math

import jax
import jax.numpy as jnp
from jax import lax
from jax.experimental import pallas as pl
from jax.experimental.pallas import tpu as pltpu
from jax.sharding import PartitionSpec as P

HD = 128
PAIR = 2
VMEM_BYTES = 60 << 20
UNIT, LANES, KEYS, WIDE = 4, 256, 128, 768
F32, BF16 = jnp.float32, jnp.bfloat16
NT = (((1,), (1,)), ((), ()))
TN = (((0,), (0,)), ((), ()))


def xor_permute(array, axis, size, mask):
    return lax.ppermute(array, axis, [(i, i ^ mask) for i in range(size)])


def attention_kernel(
    chips, tok, group, head, units, packing, layout, pos_ref, q_own, g_own, qg_rx, *refs
):
    n_in = len(packing)
    kv_in = refs[:n_in]
    dq_own, dq_oth = refs[n_in : n_in + 2]
    dkv_out = refs[n_in + 2 : n_in + 2 + len(layout)]
    qs, gs, kv, kt, acc, es, ds, ms, dqa, dqs, own_block, sent_blocks, sems, out_sems = refs[n_in + 2 + len(layout) :]
    span = PAIR * tok
    rows = UNIT * span
    width = group * HD
    chip, core = pos_ref[0], pos_ref[1]
    heads = q_own.shape[1] // (PAIR * width)
    col = pl.multiple_of((core * heads + head) * width, width)
    own = pl.multiple_of(core * tok, tok)
    oth = pl.multiple_of((1 - core) * tok, tok)
    copies = [
        (q_own.at[:, pl.ds(col, width)], qs.at[pl.ds(own, tok)]),
        (qg_rx.at[:, pl.ds(0, width)], qs.at[pl.ds(oth, tok)]),
        (g_own.at[:, pl.ds(col, width)], gs.at[pl.ds(own, tok)]),
        (qg_rx.at[:, pl.ds(width, width)], gs.at[pl.ds(oth, tok)]),
    ]
    for ref, (slots, lo) in zip(kv_in, packing):
        for i, s in enumerate(slots):
            copies.append((ref.at[pl.ds(i * span, span), pl.ds(lo, 2 * HD)], kv.at[chip ^ s]))
    started = [pltpu.make_async_copy(a, b, sems.at[i]) for i, (a, b) in enumerate(copies)]
    for c in started:
        c.start()
    acc[...] = jnp.zeros_like(acc)
    for c in started[:5]:
        c.wait()
    scale = 1.0 / math.sqrt(HD)
    log_scale = scale * math.log2(math.e)

    def turn(j, _):
        kt[j] = kv[j, :, :HD].T
        return 0

    def columns_of(u):
        return pl.ds(pl.multiple_of(u * UNIT * HD, UNIT * HD), UNIT * HD)

    def stacked(ref, u):
        wide = ref[:, columns_of(u)]
        return jnp.concatenate([wide[:, i * HD : (i + 1) * HD] for i in range(UNIT)], 0)

    def unit(u, _):
        q = stacked(qs, u)
        g = stacked(gs, u)
        qt, gt = q.T, g.T

        def scores(j, carry, masked):
            out = []
            for t, lane in enumerate(range(0, rows, LANES)):
                top, total, weighted = carry[t]
                for i, key in enumerate(range(0, span, KEYS)):
                    s = lax.dot_general(
                        kv[j, key : key + KEYS, :HD],
                        q[lane : lane + LANES],
                        NT,
                        preferred_element_type=F32,
                    ) * log_scale
                    if masked:
                        key_ids = lax.broadcasted_iota(jnp.int32, s.shape, 0) + key
                        row_ids = lax.broadcasted_iota(jnp.int32, s.shape, 1) + lane % span
                        row_ids = jnp.where(row_ids >= span, row_ids - span, row_ids)
                        s = jnp.where(key_ids <= row_ids, s, -jnp.inf)
                    dp = lax.dot_general(
                        kv[j, key : key + KEYS, HD:],
                        g[lane : lane + LANES],
                        NT,
                        preferred_element_type=F32,
                    )
                    new = jnp.maximum(top, jnp.max(s, axis=0, keepdims=True))
                    e = jnp.exp2(s - new)
                    fade = jnp.exp2(top - new)
                    es[j, key : key + KEYS, lane : lane + LANES] = e
                    ds[j, key : key + KEYS, lane : lane + LANES] = dp
                    ms[j, i : i + 1, lane : lane + LANES] = new
                    total = total * fade + jnp.sum(e, axis=0, keepdims=True)
                    weighted = weighted * fade + jnp.sum(e * dp, axis=0, keepdims=True)
                    top = new
                out.append((top, total, weighted))
            return tuple(out)

        zero = jnp.zeros((1, LANES), F32)
        start = (jnp.full((1, LANES), -jnp.inf, F32), zero, zero)
        carry = scores(chip, (start,) * (rows // LANES), True)

        @pl.when(u == 0)
        def _():
            for c in started[5:]:
                c.wait()
            lax.fori_loop(0, chip + 1, turn, 0)

        carry = lax.fori_loop(0, chip, lambda j, c: scores(j, c, False), carry)
        top, total, weighted = (jnp.concatenate(x, 1) for x in zip(*carry))
        inv = 1.0 / total
        delta = weighted * inv
        dqa[...] = jnp.zeros_like(dqa)

        def grads(j, _):
            for lane in range(0, rows, WIDE):
                at = slice(lane, lane + WIDE)
                ps, sgs = [], []
                for i, key in enumerate(range(0, span, KEYS)):
                    keys = slice(key, key + KEYS)
                    part = jnp.exp2(ms[j, i : i + 1, at] - top[:, at]) * inv[:, at]
                    p = es[j, keys, at] * part
                    ps.append(p.astype(BF16))
                    sgs.append((p * (ds[j, keys, at] - delta[:, at])).astype(BF16))
                p, sg = jnp.concatenate(ps, 0), jnp.concatenate(sgs, 0)
                acc[j, HD:] += lax.dot_general(gt[:, at], p, NT, preferred_element_type=F32)
                acc[j, :HD] += lax.dot_general(qt[:, at], sg, NT, preferred_element_type=F32)
                dqa[:, at] += jnp.dot(kt[j], sg, preferred_element_type=F32)
            return 0

        lax.fori_loop(0, chip + 1, grads, 0)
        out = (dqa[...] * scale).T.astype(BF16)
        dqs[:, columns_of(u)] = jnp.concatenate(
            [out[i * span : (i + 1) * span] for i in range(UNIT)], 1
        )
        for copy in query_copies(u):
            copy.start()
        return 0

    def query_copies(u):
        return [
            pltpu.make_async_copy(
                dqs.at[pl.ds(row, tok), columns_of(u)], ref.at[:, columns_of(u)], out_sems.at[i, u]
            )
            for i, (ref, row) in enumerate(((dq_own, own), (dq_oth, oth)))
        ]

    lax.fori_loop(0, units, unit, 0)
    leaving = [copy for u in range(units) for copy in query_copies(u)]
    starts, place = {(0,): 0}, 0
    for group_slots, _, _ in layout:
        if group_slots not in starts:
            starts[group_slots] = place
            place += len(group_slots) * span
    for n, (out, (group_slots, lo, hi)) in enumerate(zip(dkv_out, layout)):
        held = (own_block if group_slots == (0,) else sent_blocks).at[:, pl.ds(lo, hi - lo)]
        first_row = starts[group_slots]
        for i, s in enumerate(group_slots):
            j = chip ^ s
            part = pl.ds(first_row + i * span, span)

            @pl.when(j <= chip)
            def _():
                for half in range(lo, hi, HD):
                    cell = acc[j, half : half + HD]
                    cell = cell * scale if half == 0 else cell
                    held[part, half - lo : half - lo + HD] = cell.T.astype(held.dtype)

            @pl.when(j > chip)
            def _():
                held[part, :] = jnp.zeros((span, hi - lo), held.dtype)

        copy = pltpu.make_async_copy(
            held.at[pl.ds(first_row, len(group_slots) * span)], out, out_sems.at[2, n]
        )
        copy.start()
        leaving.append(copy)
    for copy in leaving:
        copy.wait()


def attention(pos, q_own, g_own, qg_rx, kv_parts, packing, head, direct):
    chips = sum(len(slots) for slots, _ in packing)
    width = qg_rx.shape[1] // 2
    tok = qg_rx.shape[0]
    span = PAIR * tok
    group = width // HD
    rows = UNIT * span
    if direct:
        layout = tuple(((s,), 0, 2 * HD) for s in range(chips))
    else:
        groups = [(0,)] + by_lowest_bit(chips)
        layout = tuple((slots, lo, lo + HD) for lo in (HD, 0) for slots in groups)
    hbm = pl.BlockSpec(memory_space=pl.ANY)
    out_shape = [jax.ShapeDtypeStruct((tok, width), BF16)] * 2 + [
        jax.ShapeDtypeStruct((len(slots) * span, hi - lo), F32 if slots == (0,) else BF16)
        for slots, lo, hi in layout
    ]
    inputs = [q_own, g_own, qg_rx, *kv_parts]
    outs = pl.pallas_call(
        functools.partial(
            attention_kernel, chips, tok, group, head, group // UNIT, packing, layout
        ),
        out_shape=out_shape,
        in_specs=[pl.BlockSpec(memory_space=pltpu.SMEM)] + [hbm] * len(inputs),
        out_specs=[hbm] * len(out_shape),
        scratch_shapes=[
            pltpu.VMEM((span, width), BF16),
            pltpu.VMEM((span, width), BF16),
            pltpu.VMEM((chips, span, 2 * HD), BF16),
            pltpu.VMEM((chips, HD, span), BF16),
            pltpu.VMEM((chips, 2 * HD, span), F32),
            pltpu.VMEM((chips, span, rows), F32),
            pltpu.VMEM((chips, span, rows), F32),
            pltpu.VMEM((chips, span // KEYS, rows), F32),
            pltpu.VMEM((HD, rows), F32),
            pltpu.VMEM((span, width), BF16),
            pltpu.VMEM((span, 2 * HD), F32),
            pltpu.VMEM(((chips - 1) * span, 2 * HD), BF16),
            pltpu.SemaphoreType.DMA((4 + chips,)),
            pltpu.SemaphoreType.DMA((3, max(len(layout), group // UNIT))),
        ],
        compiler_params=pltpu.CompilerParams(vmem_limit_bytes=VMEM_BYTES),
        cost_estimate=pl.CostEstimate(
            flops=400 * group * span * chips * span * HD, bytes_accessed=6 * span * width, transcendentals=0
        ),
        name="attention_grads",
    )(pos, *inputs)
    return outs


def product_kernel(chips, n_dp, tok, order, pos_ref, *refs):
    slots, halves, outs = refs[:n_dp], refs[n_dp : n_dp + PAIR], refs[n_dp + PAIR : -5]
    kvs, turned, *staged, out_sems = refs[-5:]
    depth = n_dp * tok
    block = staged[1].shape[0]
    flat = [s for group in order for s in group]
    for s in range(n_dp):
        kvs[pos_ref[2] ^ s] = slots[s][...]
    for at in range(PAIR):
        rows = kvs[:, at * tok : (at + 1) * tok]
        turned[at] = rows.reshape(depth, rows.shape[2]).T
    leaving = []
    for i, s in enumerate(flat):
        columns = pl.ds(pl.multiple_of((pos_ref[0] ^ s) * block, block), block)
        both = sum(
            jnp.dot(turned[at], halves[at][:, columns], preferred_element_type=F32)
            for at in range(PAIR)
        ).T
        n = next(n for n, group in enumerate(order) if s in group)
        target = outs[n].at[pl.ds(order[n].index(s) * block, block)]
        if s == 0:
            staged[1][...] = both
            source = staged[1]
        else:
            staged[0][i] = both.astype(BF16)
            source = staged[0].at[i]
        copy = pltpu.make_async_copy(source, target, out_sems.at[i])
        copy.start()
        leaving.append(copy)
    for copy in leaving:
        copy.wait()


def weight_products(pos, slots, hidden_own, hidden_oth, chips):
    n_dp = len(slots)
    span, wide = slots[0].shape
    depth, share = hidden_own.shape
    block = share // chips
    order = by_lowest_bit(chips) + [(0,)]
    anywhere = pl.BlockSpec(memory_space=pl.ANY)
    outs = pl.pallas_call(
        functools.partial(product_kernel, chips, n_dp, span // PAIR, order),
        in_specs=[pl.BlockSpec(memory_space=pltpu.SMEM)] + [pl.BlockSpec(memory_space=pltpu.VMEM)] * (n_dp + PAIR),
        out_specs=[anywhere] * len(order),
        out_shape=[
            jax.ShapeDtypeStruct((len(group) * block, wide), F32 if group == (0,) else BF16)
            for group in order
        ],
        scratch_shapes=[
            pltpu.VMEM((n_dp, span, wide), BF16),
            pltpu.VMEM((PAIR, wide, depth), BF16),
            pltpu.VMEM((chips - 1, block, wide), BF16),
            pltpu.VMEM((block, wide), F32),
            pltpu.SemaphoreType.DMA((chips,)),
        ],
        compiler_params=pltpu.CompilerParams(vmem_limit_bytes=16 << 20),
        cost_estimate=pl.CostEstimate(flops=1, bytes_accessed=1, transcendentals=0),
        name="weight_products",
    )(pos, *slots, hidden_own, hidden_oth)
    return outs[-1], list(outs[:-1])


def by_lowest_bit(chips):
    bits = chips.bit_length() - 1
    return [tuple(s for s in range(1, chips) if s & -s == 1 << i) for i in range(bits)]


def on_device(queries, keys, values, out_grad, hidden):
    tok = queries.shape[0]
    n_dp, n_ctx = lax.axis_size("dp"), lax.axis_size("ctx")
    chips = n_ctx // PAIR
    kv_heads = keys.shape[1] // HD
    own_heads = kv_heads // PAIR
    width = queries.shape[1] // kv_heads
    dp, ctx = lax.axis_index("dp"), lax.axis_index("ctx")
    chip, core = ctx // PAIR, ctx % PAIR
    pos = jnp.stack([chip, core, dp]).astype(jnp.int32)
    first = core == 0

    def swap(x):
        return xor_permute(x, "ctx", n_ctx, 1)

    def across(x, mask):
        return xor_permute(x, "ctx", n_ctx, mask * PAIR)

    def in_order(mine, theirs, axis):
        return jnp.where(
            first,
            jnp.concatenate([mine, theirs], axis),
            jnp.concatenate([theirs, mine], axis),
        )

    def columns(x, head, size):
        return lax.dynamic_slice_in_dim(x, head * size, size, 1)

    def after(x, *others):
        return lax.optimization_barrier((x, others))[0]

    def both_kv(owner):
        return jnp.concatenate(
            [columns(x, owner * own_heads + a, HD) for a in range(own_heads) for x in (keys, values)], 1
        )

    def rows_for_pair(a, queries, out_grad):
        theirs = (1 - core) * own_heads + a
        return jnp.concatenate([columns(queries, theirs, width), columns(out_grad, theirs, width)], 1)

    lowest = by_lowest_bit(chips)

    def own_first(total):
        return jnp.where(first, total, jnp.concatenate([total[tok:], total[:tok]], 0))

    def over_sequences(total):
        return [total] + [xor_permute(total, "dp", n_dp, s) for s in range(1, n_dp)]

    def product_blocks(slots, *gate):
        return weight_products(pos, after(slots, *gate), hidden_own, hidden_oth, chips)

    def core_rows(summed):
        rows = share // n_ctx
        mine = lax.dynamic_slice_in_dim(summed, core * rows, rows, 0)
        theirs = lax.dynamic_slice_in_dim(summed, (1 - core) * rows, rows, 0)
        return mine, swap(theirs)

    def step(kept, groups, i, *gate):
        groups = list(groups)
        got = after(across(groups[i].astype(BF16), 1 << i), *gate)
        size = got.shape[0] // len(lowest[i])
        for at, s in enumerate(lowest[i]):
            piece = got[at * size : (at + 1) * size].astype(F32)
            to = s ^ (1 << i)
            if to == 0:
                kept = kept + piece
            else:
                g = next(g for g in range(len(lowest)) if to in lowest[g])
                at_to = lowest[g].index(to) * size
                pieces = [groups[g][:at_to], groups[g][at_to : at_to + size].astype(F32) + piece, groups[g][at_to + size :]]
                groups[g] = jnp.concatenate([x.astype(BF16) for x in pieces if x.shape[0]], 0)
        return kept, groups

    share = hidden.shape[1] // n_dp
    bits = len(lowest)

    kept, got = both_kv(core), swap(both_kv(1 - core))
    wide = 2 * HD
    kv_local = [in_order(kept[:, i * wide : (i + 1) * wide], got[:, i * wide : (i + 1) * wide], 0) for i in range(own_heads)]

    def doubling(slots, bits, *gate):
        for bit in bits:
            slots = slots | {s ^ bit: across(after(x, *gate), bit) for s, x in slots.items()}
        return slots

    far_first = [1 << i for i in reversed(range(bits))]
    queries_, out_grad_, hidden_ = after((queries, out_grad, hidden), kv_local)
    rx, rx1 = rows_for_pair(0, queries_, out_grad_), rows_for_pair(1, queries_, out_grad_)
    shares = hidden_.reshape(tok, n_dp, share).transpose(1, 0, 2)
    slots = doubling({0: kv_local[0]}, far_first[:-1])
    near = across(kv_local[0], 1)
    forward = {s: after(slots[s], rx, shares) for s in range(2, chips, 2)}
    slots |= {1: near} | {s ^ 1: across(x, 1) for s, x in forward.items()}
    rx, rx1 = swap(rx), swap(rx1)
    hidden_own = lax.all_to_all(shares, "dp", split_axis=0, concat_axis=0, tiled=True)
    hidden_own = hidden_own.reshape(n_dp * tok, share)
    parts = [slots[s] for s in range(chips)]
    packing = tuple(((s,), 0) for s in range(chips))
    local1 = after(kv_local[1], parts)
    parts1 = [local1] + [across(local1, s) for s in range(1, chips)]
    dq_own, dq_oth, *blocks = attention(
        pos, queries, out_grad, rx, parts, packing, 0, True
    )

    moved = [blocks[0]] + [across(blocks[s], s) for s in range(1, chips)]
    rx1, parts1, hidden_own = after((rx1, parts1, hidden_own), blocks)
    hidden_oth = swap(hidden_own)
    dq_own1, dq_oth1, *blocks1 = attention(
        pos, queries, out_grad, rx1, parts1, packing, 1, False
    )
    one = sum(x.astype(F32) for x in after(moved, blocks1))
    hidden_oth, dq_oth = after((hidden_oth, dq_oth), one)

    total = own_first(one.astype(BF16))
    slots = over_sequences(total)
    size = 1 + len(lowest)
    value, key = ((blocks1[i], blocks1[i + 1 : i + size]) for i in (0, size))
    for i in range(bits - 1):
        value = step(*value, i)
        key = step(*key, i, value)
    product = product_blocks(slots, key)
    value = step(*value, bits - 1, product)
    total_v = own_first(value[0].astype(BF16))
    slots_v = over_sequences(total_v)
    key = step(*key, bits - 1, total_v)
    total_k = own_first(key[0].astype(BF16))
    slots_k = over_sequences(total_k)
    product_v = product_blocks(slots_v, total_k)
    for i in range(bits - 1):
        product = step(*product, i, product_v)
    product_k = product_blocks(slots_k, product)
    total, total_v, total_k, dq_oth, dq_oth1 = after(
        (total, total_v, total_k, dq_oth, dq_oth1), product_k[0]
    )
    for i in range(bits - 1):
        product_v = step(*product_v, i, product_k)
    for i in range(bits - 1):
        product_k = step(*product_k, i, product_v)
    product = step(*product, bits - 1, product_k)
    product_v = step(*product_v, bits - 1, product)

    def spread(one, two, lo):
        return in_order(*(jnp.concatenate([x[:, lo : lo + HD], y], 1) for x, y in zip(one, two)), 1)

    both = swap(jnp.concatenate([total[tok:], total_k[tok:], total_v[tok:]], 1))
    wide = 2 * HD
    kv_first = total[:tok], both[:, :wide]
    w_first, w_value = core_rows(product[0]), core_rows(product_v[0])
    done = (
        in_order(
            jnp.concatenate([dq_own, dq_own1], 1),
            swap(jnp.concatenate([dq_oth, dq_oth1], 1)),
            1,
        ),
        spread(kv_first, (total_k[:tok], both[:, wide : wide + HD]), 0),
        spread(kv_first, (total_v[:tok], both[:, wide + HD :]), HD),
    )
    value_weights = spread(w_first, w_value, HD)
    product_k = step(*product_k, bits - 1, done, value_weights)
    return *done, spread(w_first, core_rows(product_k[0]), 0), value_weights


def solution(mesh):
    spec = P(("dp", "ctx"), None)
    return jax.shard_map(
        on_device, mesh=mesh, in_specs=(spec,) * 5, out_specs=(spec,) * 5, check_vma=False
    )
```
